32 devices in a mesh: sec: 2 (over x), dev: 16 (over z, y, core).
Axes of the slice: x: 2, y: 2, z: 4, core: 2. Of those that a mesh axis runs over, the one named last changes fastest.
Arguments:
- hidden_in: bfloat16 [128, 7168], P(('sec', 'dev')), may hold values from -6 to 6
- expert_ids: int32 [128, 2], P(('sec', 'dev')), may hold values from 0 to 3, all different within a row; in each aligned block of 4 rows (0 to 3, 4 to 7, ...) at most 4 rows name the same one
- gate_scores: bfloat16 [128, 2], P(('sec', 'dev')), may hold values from 0.099609375 to 1
- w_gate: bfloat16 [7168, 8192], P(None, ('sec', 'dev')), may hold values from -0.0625 to 0.0625
- w_up: bfloat16 [7168, 8192], P(None, ('sec', 'dev')), may hold values from -0.0625 to 0.0625
- w_down: bfloat16 [8192, 7168], P(('sec', 'dev')), may hold values from -0.125 to 0.125
- norm_gain: float32 [7168], replicated, may hold values from 0.1 to 1.9
- w_kv: bfloat16 [7168, 576], P('dev'), may hold values from -0.0625 to 0.0625
- queries: bfloat16 [128, 64, 576], P(('sec', 'dev')), may hold values from -40 to 40
- kv_cache: bfloat16 [128, 256, 576], P(('sec', 'dev')), may hold values from -6 to 6
- lengths: int32 [128], P(('sec', 'dev')), may hold values from 2 to 256, as said below
Outputs:
- moe_out: bfloat16 [128, 7168], P(('sec', 'dev'))
- new_latent: bfloat16 [128, 576], P(('sec', 'dev'))
- attended: bfloat16 [128, 64, 512], P(('sec', 'dev'))
The draws below stay inside these ranges and needn't reach their ends.
Inputs may be any that keep to these rules, and one draw needn't show every extreme that they name: `expert_ids`: each row names 2 different experts; among the 4 rows of one device no expert is named by more than 4 rows, and some device's rows name some expert exactly 4 times in every draw. `lengths`: some rows have all 256 positions filled in every draw.
All inputs are finite; a program needn't handle non-finite values.
Results may differ from the reference program's by a relative error of at most 0.009.
Values may be sent and summed in bfloat16 or wider, within the bound.
No kernel may reach another device: no remote copies, remote signals or barrier semaphores. Data moves between devices by JAX's collectives and lax.ppermute only.
A program may use at most 128 MiB of HBM per device.

```python
import math
import jax
import jax.numpy as jnp
import numpy as np
from jax import lax

D = 7168
FF = 2048
FF_DEV = 256
HEADS = 64
KV = 512
B_DEV = 4
LMAX = 256
LAT = 576
EXPERTS = 4
TOPK = 2
CAP = 4
ROWS = 128


def shared_cache(key):
    base = jnp.clip(jax.random.normal(jax.random.fold_in(key, 11), (ROWS, LMAX, LAT), jnp.float32), -5.0, 5.0)
    return base


def draw_kv_cache(key, part):
    return shared_cache(key).astype(jnp.bfloat16)


def draw_queries(key, part):
    query_vals = jnp.clip(jax.random.normal(jax.random.fold_in(key, 13), (ROWS, HEADS, LAT), jnp.float32), -5.0, 5.0)
    return query_vals.astype(jnp.bfloat16)


def draw_lengths(key, part):
    drawn = jax.random.randint(jax.random.fold_in(key, 21), (ROWS,), 2, LMAX + 1, dtype=jnp.int32)
    return jnp.where(jnp.arange(ROWS) % 64 == 0, LMAX, drawn).astype(jnp.int32)


def steps_of(stream_key, shape, pieces, smallest, high):
    def one(dim, blocks):
        draws = jax.random.uniform(jax.random.fold_in(jax.random.fold_in(stream_key, 6), dim), (blocks,), jnp.float32, smallest / len(pieces), high / len(pieces))
        return jnp.repeat(jnp.exp(draws), shape[dim] // blocks).reshape((-1,) + (1,) * (len(shape) - dim - 1))

    gain = one(*pieces[0])
    for cut in pieces[1:]:
        gain = gain * one(*cut)
    return gain


def routed_block(rng, own, number, rows, count, top, reach, skew):
    order = jax.random.permutation(rng, count)
    heavy_load, usual = load_shares(count, rows * top, reach, skew, True), load_shares(count, rows * top, reach, skew, False)
    places = jnp.arange(count)

    def named(sizes, rotation):
        used = int((sizes > 0).sum())
        fixed = max(1, used // 4)
        shifted = fixed + (places - fixed + rotation * (used - fixed)) % max(1, count - fixed)
        return jnp.zeros((count,), jnp.int32).at[order[jnp.where(places < fixed, places, shifted)]].set(jnp.asarray(sizes, jnp.int32))

    sizes = jnp.where(number % 4 == 0, named(heavy_load, number // 4), named(usual, number - number // 4 - 1))
    mixed = jax.random.permutation(jax.random.fold_in(own, 3), count)
    source_of, sink = mixed[0:count // 2 * 2:2], mixed[1:count // 2 * 2:2]
    margin = jnp.minimum(sizes[source_of] - 1, reach - sizes[sink]) // 2
    margin = jnp.where((source_of == order[0]) | (sink == order[0]) | (sizes[sink] == 0), 0, jnp.maximum(margin, 0))
    shifted = jax.random.randint(jax.random.fold_in(own, 4), (count // 2,), 0, 1 << 20) % (margin + 1)
    sizes = sizes.at[source_of].add(-shifted).at[sink].add(shifted)
    members = jnp.searchsorted(jnp.cumsum(sizes), jnp.arange(rows * top), side="right").astype(jnp.int32)
    table = members.reshape(top, rows).T
    table = table[jax.random.permutation(jax.random.fold_in(own, 1), rows)]
    rotation = jax.random.randint(jax.random.fold_in(own, 2), (rows, 1), 0, top)
    return jnp.take_along_axis(table, (jnp.arange(top)[None, :] + rotation) % top, axis=1)


def load_shares(count, total, reach, lean, full):
    weights = [(1 << 20) // math.isqrt(rank ** lean) + 1 for rank in range(1, count + 1)]
    largest = reach if full else min(reach, max(-(-total // count), total * weights[0] // sum(weights)))
    least = 1 if total - largest >= count - 1 else 0
    counts, surplus = [largest] + [least] * (count - 1), total - largest - least * (count - 1)
    while surplus > 0:
        movable = [i for i in range(1, count) if counts[i] < largest] or [i for i in range(1, count) if counts[i] < reach]
        pool, left = sum([weights[i] for i in movable]), surplus
        for i in movable:
            more = min(reach - counts[i], max(1, left * weights[i] // pool), surplus)
            counts[i] = counts[i] + more
            surplus = surplus - more
    return np.array(counts)


def normal_values(rng, extent, width, limit, pieces=(), kind=jnp.bfloat16):
    factor_of = steps_of(rng, extent, pieces, -0.22, 0.18) if pieces else 1.0
    entries = jax.random.normal(rng, extent, jnp.float32) * width * factor_of
    return jnp.minimum(jnp.maximum(entries, -limit), limit).astype(kind)


def setup_inputs(seed: int = 0) -> dict:
    streams_of = jax.random.split(jax.random.key(seed), 12)
    hidden_in = normal_values(streams_of[0], (ROWS, D), 1.0, 6.0, ((0, 32),))
    expert_ids_keys = jax.random.split(jax.random.fold_in(streams_of[1], 1), ROWS // B_DEV)
    expert_ids_turns = jax.random.permutation(jax.random.fold_in(streams_of[1], 3), ROWS // B_DEV)
    expert_ids = jax.vmap(lambda own, number: routed_block(jax.random.fold_in(streams_of[1], 2), own, number, B_DEV, EXPERTS, TOPK, CAP, 2))(expert_ids_keys, expert_ids_turns).reshape((ROWS, TOPK))
    gate_scores = jnp.clip(jnp.exp(math.log(1.0) - 2.306499 * jax.random.uniform(streams_of[2], (ROWS, TOPK), jnp.float32) ** steps_of(streams_of[2], (ROWS, TOPK), ((0, 32),), -0.2, 0.2)), 0.099609375, 1.0).astype(jnp.bfloat16)
    w_gate = normal_values(streams_of[3], (D, EXPERTS * FF), D ** -0.5, 0.0625, ((1, 32),))
    w_up = normal_values(streams_of[4], (D, EXPERTS * FF), D ** -0.5, 0.0625, ((1, 32),))
    w_down = normal_values(streams_of[5], (EXPERTS * FF, D), FF ** -0.5, 0.125, ((0, 32),))
    norm_gain = jnp.clip(1.0 + 0.18 * jax.random.normal(streams_of[6], (D,), jnp.float32), 0.1, 1.9)
    w_kv = normal_values(streams_of[7], (D, LAT), D ** -0.5, 0.0625, ((0, 16),))
    queries = draw_queries(jax.random.fold_in(streams_of[11], 71), 0)
    kv_cache = draw_kv_cache(jax.random.fold_in(streams_of[11], 71), 0)
    lengths = draw_lengths(jax.random.fold_in(streams_of[11], 71), 0)
    return dict(hidden_in=hidden_in, expert_ids=expert_ids, gate_scores=gate_scores, w_gate=w_gate, w_up=w_up, w_down=w_down, norm_gain=norm_gain, w_kv=w_kv, queries=queries, kv_cache=kv_cache, lengths=lengths)


score_scale = 192.0 ** (-0.5)
norm_eps = 1e-06

def attend(queries, kv_cache, lengths, latent_new):
    length_max = kv_cache.shape[1]
    scores = jnp.einsum('bhl,bpl->bhp', queries.astype(jnp.float32), kv_cache.astype(jnp.float32)) * score_scale
    visible = jnp.arange(length_max, dtype=jnp.int32)[None, None, :] < lengths[:, None, None]
    scores = jnp.where(visible, scores, -1e+30)
    own_score = jnp.einsum('bhl,bl->bh', queries.astype(jnp.float32), latent_new.astype(jnp.float32)) * score_scale
    peak = jnp.maximum(lax.optimization_barrier(jnp.max(scores, axis=2)), own_score)
    spread = jnp.exp(scores - peak[:, :, None])
    own_weight = jnp.exp(own_score - peak)
    denominator = lax.optimization_barrier(jnp.sum(spread, axis=2)) + own_weight
    cache_weights = (spread / denominator[:, :, None]).astype(jnp.bfloat16)
    own_prob = (own_weight / denominator).astype(jnp.bfloat16)
    values = kv_cache[:, :, :KV]
    combined = jnp.einsum('bhp,bpv->bhv', cache_weights.astype(jnp.float32), values.astype(jnp.float32))
    combined = combined + own_prob.astype(jnp.float32)[:, :, None] * latent_new[:, None, :KV].astype(jnp.float32)
    return combined.astype(jnp.bfloat16)

def attend_block(block_parts):
    return attend(block_parts[0], block_parts[1], block_parts[2], block_parts[3])

def reference(hidden_in, expert_ids, gate_scores, w_gate, w_up, w_down, norm_gain, w_kv, queries, kv_cache, lengths):
    slot_count = CAP * ROWS // B_DEV
    shard_count = FF // FF_DEV
    weights = gate_scores.astype(jnp.float32)
    weights = weights / lax.optimization_barrier(jnp.sum(weights, axis=1, keepdims=True))
    padded = jnp.concatenate([hidden_in, jnp.zeros((1, D), jnp.bfloat16)], axis=0)

    def expert_step(totals, expert):
        matches = expert_ids == expert
        chosen = jnp.any(matches, axis=1)
        row_weight = lax.optimization_barrier(jnp.sum(jnp.where(matches, weights, 0.0), axis=1))
        slot_rows = jnp.nonzero(chosen, size=slot_count, fill_value=ROWS)[0].astype(jnp.int32)
        gathered = padded[slot_rows]
        start = (expert * FF).astype(jnp.int32)
        gate_cols = lax.dynamic_slice_in_dim(w_gate, start, FF, 1)
        up_cols = lax.dynamic_slice_in_dim(w_up, start, FF, 1)
        down_rows = lax.dynamic_slice_in_dim(w_down, start, FF, 0)
        gate_act = jnp.dot(gathered, gate_cols, preferred_element_type=jnp.float32)
        up_act = jnp.dot(gathered, up_cols, preferred_element_type=jnp.float32)
        hidden = (jax.nn.silu(gate_act) * up_act).astype(jnp.bfloat16)
        expert_out = jnp.zeros((slot_count, D), jnp.float32)
        for shard in range(shard_count):
            first_col = shard * FF_DEV
            piece = jnp.dot(hidden[:, first_col:first_col + FF_DEV], down_rows[first_col:first_col + FF_DEV], preferred_element_type=jnp.float32).astype(jnp.bfloat16)
            piece = lax.optimization_barrier(piece)
            expert_out = expert_out + piece.astype(jnp.float32)
        scale_rows = jnp.concatenate([row_weight, jnp.zeros((1,), jnp.float32)])[slot_rows]
        totals = totals.at[slot_rows].add(scale_rows[:, None] * expert_out, mode='drop')
        return (totals, None)
    mixture, unused = lax.scan(expert_step, jnp.zeros((ROWS, D), jnp.float32), jnp.arange(EXPERTS, dtype=jnp.int32))
    moe_out = (hidden_in.astype(jnp.float32) + mixture).astype(jnp.bfloat16)
    widened = moe_out.astype(jnp.float32)
    normed = (widened * lax.rsqrt(lax.optimization_barrier(jnp.mean(widened * widened, axis=1, keepdims=True)) + norm_eps) * norm_gain).astype(jnp.bfloat16)
    new_latent = jnp.dot(normed, w_kv, preferred_element_type=jnp.float32).astype(jnp.bfloat16)
    blocks = ROWS // B_DEV
    attended = lax.map(attend_block, (queries.reshape(blocks, B_DEV, HEADS, LAT), kv_cache.reshape(blocks, B_DEV, LMAX, LAT), lengths.reshape(blocks, B_DEV), new_latent.reshape(blocks, B_DEV, LAT)))
    attended = attended.reshape(ROWS, HEADS, KV)
    return (moe_out, new_latent, attended)
```

```python
import jax
import jax.numpy as jnp
from jax import lax
from jax.experimental import pallas as pl
from jax.experimental.pallas import tpu as pltpu
from jax.sharding import PartitionSpec as P

FF = 2048
KV = 512
LANES = 128

score_scale = 192.0 ** (-0.5)
norm_eps = 1e-06


def swap(x, bit):
    if bit == "sec":
        return lax.ppermute(x, "sec", [(i, i ^ 1) for i in range(lax.axis_size("sec"))])
    return lax.ppermute(x, "dev", [(i, i ^ (1 << bit)) for i in range(lax.axis_size("dev"))])


def total(kept, received):
    return (kept.astype(jnp.float32) + received.astype(jnp.float32)).astype(jnp.bfloat16)


def flipped(x, rows):
    blocks = x.reshape(-1, 2, rows, x.shape[1])
    return jnp.concatenate([blocks[:, 1:], blocks[:, :1]], axis=1).reshape(x.shape)


def cache_part(queries, kv_cache, lengths):
    scores = (
        jnp.einsum("bhl,bpl->bhp", queries, kv_cache, preferred_element_type=jnp.float32)
        * score_scale
    )
    visible = jnp.arange(kv_cache.shape[1], dtype=jnp.int32)[None, None, :] < lengths[:, None, None]
    scores = jnp.where(visible, scores, -1e30)
    peak = jnp.max(scores, axis=2)
    spread = jnp.exp(scores - peak[:, :, None])
    combined = jnp.einsum(
        "bhp,bpv->bhv",
        spread.astype(jnp.bfloat16),
        kv_cache[:, :, :KV],
        preferred_element_type=jnp.float32,
    )
    return peak, jnp.sum(spread, axis=2), combined


def own_part(queries, latent, peak, denominator, combined):
    own_score = (
        jnp.einsum("bhl,bl->bh", queries, latent, preferred_element_type=jnp.float32) * score_scale
    )
    top = jnp.maximum(peak, own_score)
    shrink = jnp.exp(peak - top)
    own_weight = jnp.exp(own_score - top)
    scale = 1.0 / (denominator * shrink + own_weight)
    own_prob = (own_weight * scale).astype(jnp.bfloat16).astype(jnp.float32)
    value = latent[:, None, :KV].astype(jnp.float32)
    return (combined * (shrink * scale)[:, :, None] + own_prob[:, :, None] * value).astype(
        jnp.bfloat16
    )


def gather_rows(hidden_in, expert_ids, gate_scores, high, w_kv):
    width = hidden_in.shape[1]
    picks = expert_ids.shape[1]
    half = width // 2
    x = hidden_in
    info = jnp.concatenate([expert_ids.astype(jnp.bfloat16), gate_scores], axis=1)
    info = jnp.pad(info, ((0, 0), (0, LANES - 2 * picks)))
    w_low = swap(w_kv, 1)
    for bit in reversed(high):
        x, info = (jnp.concatenate([v, swap(v, bit)], axis=0) for v in (x, info))
    a, b = x[:, :half], x[:, half:]
    group = (a, b)
    b = jnp.concatenate([b, info], axis=1)
    a, b = (jnp.concatenate([v, swap(v, 2)], axis=0) for v in (a, b))
    a, b, w_low = lax.optimization_barrier((a, b, w_low))
    w_mid = swap(w_kv, 2)
    a_low, b_sec = swap(a, 1), swap(b, "sec")
    a_sec = swap(jnp.concatenate([a, a_low], axis=0), "sec")
    b_low = swap(jnp.concatenate([b, b_sec], axis=0), 1)
    w_both = swap(w_low, 2)
    a_all = (a, a_low, a_sec)
    b_all = (b, b_sec, b_low)
    a_all += tuple(swap(v, 0) for v in a_all)
    b_all += tuple(swap(v, 0) for v in b_all)
    return group, a_all, b_all, (w_kv, w_low, w_mid, w_both)


def experts_kernel(picks, expert_ref, *refs):
    a_refs, b_refs = refs[:6], refs[6:12]
    gate_ref, up_ref, down_ref, keep_a, keep_b, send_a, send_b, x_ref, info_ref = refs[12:]
    half = a_refs[0].shape[1]
    size = a_refs[0].shape[0]
    rows = 8 * size
    for side in range(2):
        first = side * 4 * size
        own, low, sec = a_refs[3 * side : 3 * side + 3]
        x_ref[first : first + size, :half] = own[...]
        x_ref[first + size : first + 2 * size, :half] = low[...]
        x_ref[first + 2 * size : first + 4 * size, :half] = sec[...]
        own, sec, low = b_refs[3 * side : 3 * side + 3]
        places = ((own, 0, 0), (low, 0, 1), (sec, 0, 2), (low, size, 3))
        for ref, start, slot in places:
            to = pl.ds(first + slot * size, size)
            x_ref[to, half:] = ref[start : start + size, :half]
            info_ref[to, :] = ref[start : start + size, half:].astype(jnp.float32)
    info = info_ref[...]
    lane = lax.broadcasted_iota(jnp.int32, info.shape, 1)
    scores = jnp.where(lane < picks, pltpu.roll(info, LANES - picks, 1), 0.0)
    named = jnp.where(info == expert_ref[0].astype(jnp.float32), scores, 0.0)
    share = jnp.sum(named, axis=1, keepdims=True) / jnp.sum(scores, axis=1, keepdims=True)
    depth = 1024
    gate_act = jnp.zeros((rows, gate_ref.shape[1]), jnp.float32)
    up_act = jnp.zeros((rows, gate_ref.shape[1]), jnp.float32)
    for k in range(0, 2 * half, depth):
        x = x_ref[:, k : k + depth]
        gate_act += jnp.dot(x, gate_ref[k : k + depth, :], preferred_element_type=jnp.float32)
        up_act += jnp.dot(x, up_ref[k : k + depth, :], preferred_element_type=jnp.float32)
    hidden = (gate_act / (1.0 + jnp.exp(-gate_act)) * up_act).astype(jnp.bfloat16)
    cols = 512
    for first, kept, sent in ((0, keep_a, send_a), (half, keep_b, send_b)):
        for c in range(0, half, cols):
            partial = jnp.dot(
                hidden,
                down_ref[:, first + c : first + c + cols],
                preferred_element_type=jnp.float32,
            )
            partial = (partial * share).astype(jnp.bfloat16)
            kept[:, c : c + cols] = partial[: rows // 2]
            sent[:, c : c + cols] = partial[rows // 2 :]


def experts(a_all, b_all, picks, expert, w_gate, w_up, w_down):
    size, half = a_all[0].shape
    out = jax.ShapeDtypeStruct((4 * size, half), jnp.bfloat16)
    vmem = pl.BlockSpec(memory_space=pltpu.VMEM)
    return pl.pallas_call(
        lambda *refs: experts_kernel(picks, *refs),
        out_shape=(out,) * 4,
        in_specs=[pl.BlockSpec(memory_space=pltpu.SMEM)] + [vmem] * 15,
        out_specs=[vmem] * 4,
        scratch_shapes=[
            pltpu.VMEM((8 * size, 2 * half), jnp.bfloat16),
            pltpu.VMEM((8 * size, LANES), jnp.float32),
        ],
        compiler_params=pltpu.CompilerParams(vmem_limit_bytes=48 << 20),
        name="experts",
    )(expert.reshape(1), *a_all, *b_all, w_gate, w_up, w_down)


def experts_wide(a_all, b_all, picks, expert, w_gate, w_up, w_down):
    size, half = a_all[0].shape
    b_all = [
        v
        for own, sec, low in (b_all[:3], b_all[3:])
        for v in (own, low[:size], sec, low[size:])
    ]
    a, b = jnp.concatenate(a_all, axis=0), jnp.concatenate(b_all, axis=0)
    info = b[:, half:].astype(jnp.float32)
    scores = info[:, picks : 2 * picks]
    named = jnp.where(info[:, :picks] == expert.astype(jnp.float32), scores, 0.0)
    share = jnp.sum(named, axis=1, keepdims=True) / jnp.sum(scores, axis=1, keepdims=True)
    x = jnp.concatenate([a, b[:, :half]], axis=1)
    gate_act = jnp.dot(x, w_gate, preferred_element_type=jnp.float32)
    up_act = jnp.dot(x, w_up, preferred_element_type=jnp.float32)
    hidden = (jax.nn.silu(gate_act) * up_act).astype(jnp.bfloat16)
    partial = jnp.dot(hidden, w_down, preferred_element_type=jnp.float32)
    partial = (share * partial).astype(jnp.bfloat16)
    rows = 4 * size
    return partial[:rows, :half], partial[:rows, half:], partial[rows:, :half], partial[rows:, half:]


def scatter_rows(keep_a, keep_b, send_a, send_b):
    rows = keep_a.shape[0] // 2
    quarter = rows // 2
    a, b = total(keep_a, swap(send_a, 0)), total(keep_b, swap(send_b, 0))
    a_in = swap(a[rows:], "sec")
    b_in = swap(jnp.concatenate([b[quarter:rows], b[rows + quarter :]], axis=0), 1)
    a = total(a[:rows], a_in)
    b = total(jnp.concatenate([b[:quarter], b[rows : rows + quarter]], axis=0), b_in)
    a_in, b_in = swap(a[quarter:], 1), swap(b[quarter:], "sec")
    a, b = total(a[:quarter], a_in), total(b[:quarter], b_in)
    rows = quarter // 2
    return tuple(total(v[:rows], swap(v[rows:], 2)) for v in (a, b))


def latent_parts_kernel(
    place_ref, a_ref, b_ref, in_ref, res_a, res_b, gain_ref, *refs
):
    slices = refs[:8]
    sums_ref, sums_out, moe_ref, moe_out, piece_ref = refs[8:]
    rows, half = a_ref.shape
    own = rows // 2
    piece, lat = slices[0].shape
    upper = place_ref[0] == 1
    kept = jnp.where(upper, b_ref[...], a_ref[...]).astype(jnp.float32)
    residual = jnp.where(upper, res_b[...], res_a[...]).astype(jnp.float32)
    moe = (residual + (kept + in_ref[...].astype(jnp.float32))).astype(jnp.bfloat16)
    moe_ref[...] = moe[:own]
    moe_out[...] = moe[own:]
    widened = moe.astype(jnp.float32)
    scaled = widened * gain_ref[pl.ds(place_ref[0], 1), :]
    for p in range(8):
        piece_ref[p] = scaled[:, p * piece : (p + 1) * piece]
    sums = jnp.zeros((rows, lat), jnp.float32)
    for slot, w_ref in enumerate(slices):
        flips = ((slot & 1) << 1) | ((slot & 2) << 1) | (slot >> 2)
        x = piece_ref[place_ref[1] ^ flips].astype(jnp.bfloat16)
        sums += jnp.dot(x, w_ref[...], preferred_element_type=jnp.float32)
    squares = jnp.sum(widened * widened, axis=1, keepdims=True)
    tail = jnp.broadcast_to(squares, (rows, LANES))
    for ref, first in ((sums_ref, 0), (sums_out, own)):
        ref[:, :lat] = sums[first : first + own]
        ref[:, lat:] = tail[first : first + own, : ref.shape[1] - lat]


def latent_parts(place, a, b, received, res_a, res_b, gain, slices):
    rows, half = a.shape
    piece, lat = slices[0].shape
    own = rows // 2
    vmem = pl.BlockSpec(memory_space=pltpu.VMEM)
    padded = -(-(lat + 1) // LANES) * LANES
    sums = jax.ShapeDtypeStruct((own, padded), jnp.float32)
    moe = jax.ShapeDtypeStruct((own, half), jnp.bfloat16)
    return pl.pallas_call(
        latent_parts_kernel,
        out_shape=(sums, sums, moe, moe),
        in_specs=[pl.BlockSpec(memory_space=pltpu.SMEM)] + [vmem] * 14,
        out_specs=[vmem] * 4,
        scratch_shapes=[pltpu.VMEM((8, rows, piece), jnp.float32)],
        compiler_params=pltpu.CompilerParams(vmem_limit_bytes=32 << 20),
        name="latent_parts",
    )(place, a, b, received, res_a, res_b, gain.reshape(2, half), *slices)


def latent_parts_wide(device, high, mixture, residual, own_rows, norm_gain, slices):
    for bit in reversed(high[:-1]):
        part = mixture.shape[1] // 2
        upper = ((device >> bit) & 1) == 1
        lo, hi = mixture[:, :part], mixture[:, part:]
        sent = flipped(jnp.where(upper, lo, hi), own_rows << (high[-1] - bit))
        mixture = total(jnp.where(upper, hi, lo), swap(sent, bit))
        residual = jnp.where(upper, residual[:, part:], residual[:, :part])
    part = mixture.shape[1]
    moe = (residual.astype(jnp.float32) + mixture.astype(jnp.float32)).astype(jnp.bfloat16)
    widened = moe.astype(jnp.float32)
    gain = lax.dynamic_slice_in_dim(norm_gain, (device >> 3) * part, part, axis=0)
    squares = jnp.sum(widened * widened, axis=1, keepdims=True)
    scaled = (widened * gain).astype(jnp.bfloat16)
    slices = jnp.stack(slices)
    piece = slices.shape[1]
    latent = jnp.zeros((moe.shape[0], slices.shape[2]), jnp.float32)
    for p in range(8):
        flips = (device & 7) ^ p
        slot = ((flips >> 1) & 1) | ((flips >> 1) & 2) | ((flips & 1) << 2)
        weight = lax.dynamic_index_in_dim(slices, slot, axis=0, keepdims=False)
        latent += jnp.dot(
            scaled[:, p * piece : (p + 1) * piece], weight, preferred_element_type=jnp.float32
        )
    sums = jnp.concatenate([latent, squares], axis=1)
    for bit in high:
        rows = sums.shape[0] // 2
        sums = sums[:rows] + swap(sums[rows:], bit)
    for bit in high:
        rows = moe.shape[0] // 2
        upper = ((device >> bit) & 1) == 1
        kept, received = moe[:rows], swap(moe[rows:], bit)
        moe = jnp.where(
            upper,
            jnp.concatenate([received, kept], axis=1),
            jnp.concatenate([kept, received], axis=1),
        )
    return sums, moe


def per_device(
    hidden_in,
    expert_ids,
    gate_scores,
    w_gate,
    w_up,
    w_down,
    norm_gain,
    w_kv,
    queries,
    kv_cache,
    lengths,
):
    devices = lax.axis_size("dev")
    device = lax.axis_index("dev")
    shard_count = FF // w_gate.shape[1]
    expert = lax.axis_index("sec") * (devices // shard_count) + device // shard_count
    high = range(3, devices.bit_length() - 1)
    own_rows, width = hidden_in.shape

    picks = expert_ids.shape[1]
    half = width // 2

    group, a_all, b_all, slices = gather_rows(hidden_in, expert_ids, gate_scores, high, w_kv)
    peak, denominator, combined = cache_part(queries, kv_cache, lengths)
    run = experts if len(high) == 1 else experts_wide
    partial = run(a_all, b_all, picks, expert, w_gate, w_up, w_down)
    partial, slices = lax.optimization_barrier((partial, slices))
    a, b = scatter_rows(*partial)
    slices += tuple(swap(v, 0) for v in slices)

    upper = (device >> high[-1]) & 1
    sent = flipped(jnp.where(upper == 1, a, b), own_rows)
    received = swap(sent, high[-1])
    if len(high) == 1:
        place = jnp.stack([upper, device & 7])
        sums, sums_out, moe, moe_out = latent_parts(place, a, b, received, *group, norm_gain, slices)
        sums = sums + swap(sums_out, high[0])
        moe_in = swap(moe_out, high[0])
        moe = jnp.concatenate([moe, moe_in], axis=1)
        swapped = jnp.concatenate([moe_in, moe[:, :half]], axis=1)
        moe = jnp.where(upper == 1, swapped, moe)
    else:
        mixture = total(jnp.where(upper == 1, b, a), received)
        residual = jnp.where(upper == 1, group[1], group[0])
        sums, moe = latent_parts_wide(device, high, mixture, residual, own_rows, norm_gain, slices)
    lat = w_kv.shape[1]
    inverse = lax.rsqrt(sums[:, lat : lat + 1] / width + norm_eps)
    new_latent = (sums[:, :lat] * inverse).astype(jnp.bfloat16)
    attended = own_part(queries, new_latent, peak, denominator, combined)
    return (moe, new_latent, attended)


def solution(mesh):
    in_specs = (
        P(("sec", "dev"), None),
        P(("sec", "dev"), None),
        P(("sec", "dev"), None),
        P(None, ("sec", "dev")),
        P(None, ("sec", "dev")),
        P(("sec", "dev"), None),
        P(),
        P("dev", None),
        P(("sec", "dev"), None, None),
        P(("sec", "dev"), None, None),
        P(("sec", "dev")),
    )
    out_specs = (P(("sec", "dev"), None), P(("sec", "dev"), None), P(("sec", "dev"), None, None))
    return jax.shard_map(
        per_device, mesh=mesh, in_specs=in_specs, out_specs=out_specs, check_vma=False
    )
```

```python
import jax
import jax.numpy as jnp
from jax import lax
from jax.experimental import pallas as pl
from jax.experimental.pallas import tpu as pltpu
from jax.sharding import PartitionSpec as P

FF = 2048
KV = 512
LANES = 128

score_scale = 192.0 ** (-0.5)
norm_eps = 1e-06


def swap(x, bit):
    if bit == "sec":
        return lax.ppermute(x, "sec", [(i, i ^ 1) for i in range(lax.axis_size("sec"))])
    return lax.ppermute(x, "dev", [(i, i ^ (1 << bit)) for i in range(lax.axis_size("dev"))])


def wide_total(kept, received):
    return kept.astype(jnp.float32) + received.astype(jnp.float32)


def total(kept, received):
    return wide_total(kept, received).astype(jnp.bfloat16)


def flipped(x, rows):
    blocks = x.reshape(-1, 2, rows, x.shape[1])
    return jnp.concatenate([blocks[:, 1:], blocks[:, :1]], axis=1).reshape(x.shape)


def cache_kernel(lengths_ref, q_ref, kv_ref, stats_ref, out_ref):
    heads, count = q_ref.shape[1], kv_ref.shape[2]
    lane = lax.broadcasted_iota(jnp.int32, (heads, LANES), 1)
    position = lax.broadcasted_iota(jnp.int32, (heads, count), 1)
    for row in range(q_ref.shape[0]):
        scores = jnp.dot(q_ref[row], kv_ref[row], preferred_element_type=jnp.float32) * score_scale
        scores = jnp.where(position < lengths_ref[row], scores, -1e30)
        peak = jnp.max(scores, axis=1, keepdims=True)
        spread = jnp.exp(scores - peak)
        denominator = jnp.sum(spread, axis=1, keepdims=True)
        out_ref[row] = lax.dot_general(
            spread.astype(jnp.bfloat16),
            kv_ref[row, :KV, :],
            (((1,), (1,)), ((), ())),
            preferred_element_type=jnp.float32,
        )
        stats_ref[row] = jnp.where(lane == 0, peak, denominator)


def cache_part(queries, kv_cache, lengths):
    rows, heads = queries.shape[:2]
    vmem = pl.BlockSpec(memory_space=pltpu.VMEM)
    return pl.pallas_call(
        cache_kernel,
        out_shape=(
            jax.ShapeDtypeStruct((rows, heads, LANES), jnp.float32),
            jax.ShapeDtypeStruct((rows, heads, KV), jnp.float32),
        ),
        in_specs=[pl.BlockSpec(memory_space=pltpu.SMEM), vmem, vmem],
        out_specs=[vmem] * 2,
        compiler_params=pltpu.CompilerParams(vmem_limit_bytes=8 << 20),
        cost_estimate=pl.CostEstimate(
            flops=4 * queries.size * kv_cache.shape[1],
            bytes_accessed=2 * kv_cache.size,
            transcendentals=0,
        ),
        name="cache_part",
    )(lengths, queries, jnp.swapaxes(kv_cache, 1, 2))


def finish_kernel(width, sums_ref, in_ref, q_ref, stats_ref, part_ref, latent_ref, out_ref):
    lat = q_ref.shape[2]
    sums = sums_ref[...] + in_ref[...]
    inverse = lax.rsqrt(sums[:, lat : lat + 1] / width + norm_eps)
    rounded = (sums[:, :lat] * inverse).astype(jnp.bfloat16)
    latent_ref[...] = rounded
    latent = rounded.astype(jnp.float32)
    for row in range(q_ref.shape[0]):
        own = latent[row : row + 1]
        own_score = jnp.sum(q_ref[row].astype(jnp.float32) * own, axis=1, keepdims=True) * score_scale
        peak, denominator = stats_ref[row, :, 0:1], stats_ref[row, :, 1:2]
        top = jnp.maximum(peak, own_score)
        shrink = jnp.exp(peak - top)
        own_weight = jnp.exp(own_score - top)
        scale = 1.0 / (denominator * shrink + own_weight)
        own_prob = (own_weight * scale).astype(jnp.bfloat16).astype(jnp.float32)
        value = part_ref[row] * (shrink * scale) + own_prob * own[:, :KV]
        out_ref[row] = value.astype(jnp.bfloat16)


def finish(width, sums, sums_in, queries, stats, combined):
    rows, heads, lat = queries.shape
    vmem = pl.BlockSpec(memory_space=pltpu.VMEM)
    return pl.pallas_call(
        lambda *refs: finish_kernel(width, *refs),
        out_shape=(
            jax.ShapeDtypeStruct((rows, lat), jnp.bfloat16),
            jax.ShapeDtypeStruct((rows, heads, KV), jnp.bfloat16),
        ),
        in_specs=[vmem] * 5,
        out_specs=[vmem] * 2,
        compiler_params=pltpu.CompilerParams(vmem_limit_bytes=8 << 20),
        name="finish",
    )(sums, sums_in, queries, stats, combined)


def gather_rows(hidden_in, expert_ids, gate_scores, high, w_kv):
    width = hidden_in.shape[1]
    picks = expert_ids.shape[1]
    half = width // 2
    x = hidden_in
    info = jnp.concatenate([expert_ids.astype(jnp.bfloat16), gate_scores], axis=1)
    info = jnp.pad(info, ((0, 0), (0, LANES - 2 * picks)))
    w_low = swap(w_kv, 1)
    for bit in reversed(high):
        x, info = (jnp.concatenate([v, swap(v, bit)], axis=0) for v in (x, info))
    a, b = x[:, :half], x[:, half:]
    group = (a, b)
    b = jnp.concatenate([b, info], axis=1)
    a, b = (jnp.concatenate([v, swap(v, 2)], axis=0) for v in (a, b))
    a, b, w_own = lax.optimization_barrier((a, b, w_kv))
    w_mid = swap(w_own, 2)
    a_low, b_sec = swap(a, 1), swap(b, "sec")
    a, b = jnp.concatenate([a, a_low], axis=0), jnp.concatenate([b, b_sec], axis=0)
    a_sec, b_low = swap(a, "sec"), swap(b, 1)
    *a_all, w_low = lax.optimization_barrier((a, a_sec, w_low))
    w_both = swap(w_low, 2)
    a_all, b_all = tuple(a_all), (b, b_low)
    a_all += tuple(swap(v, 0) for v in a_all)
    b_all += tuple(swap(v, 0) for v in b_all)
    return group, a_all, b_all, (w_own, w_low, w_mid, w_both)


CHUNK = 512


def experts_kernel(picks, expert_ref, *refs):
    a_refs, b_refs, w_refs, outs = refs[:4], refs[4:8], refs[8:11], refs[11:15]
    gate_ref, up_ref, down_ref, sems = refs[15:]
    keep_a, keep_b, send_a, send_b = outs
    size, half = a_refs[0].shape
    size //= 2
    moves = []
    for part in (pl.ds(0, half), pl.ds(half, half)):
        moves.append((w_refs[0].at[part], gate_ref.at[part]))
        moves.append((w_refs[1].at[part], up_ref.at[part]))
    for part in (pl.ds(0, half), pl.ds(half, half)):
        moves.append((w_refs[2].at[:, part], down_ref.at[:, part]))
    copies = [pltpu.make_async_copy(*move, sems.at[i]) for i, move in enumerate(moves)]
    for copy in copies:
        copy.start()

    def rows_of(part, cols):
        if part == 0:
            return jnp.concatenate([ref[:, cols] for ref in a_refs], axis=0)
        blocks = []
        for side in range(2):
            early, late = b_refs[2 * side][:, cols], b_refs[2 * side + 1][:, cols]
            blocks += [early[:size], late[:size], early[size:], late[size:]]
        return jnp.concatenate(blocks, axis=0)

    info = rows_of(1, slice(half, half + LANES)).astype(jnp.float32)
    rows, hid = info.shape[0], gate_ref.shape[1]
    lane = lax.broadcasted_iota(jnp.int32, info.shape, 1)
    scores = jnp.where(lane < picks, pltpu.roll(info, LANES - picks, 1), 0.0)
    named = jnp.where(info == expert_ref[0].astype(jnp.float32), scores, 0.0)
    share = jnp.sum(named, axis=1, keepdims=True) / jnp.sum(scores, axis=1, keepdims=True)
    gate_act = jnp.zeros((rows, hid), jnp.float32)
    up_act = jnp.zeros((rows, hid), jnp.float32)
    for part in range(2):
        copies[2 * part].wait()
        copies[2 * part + 1].wait()
        for k in range(0, half, CHUNK):
            x = rows_of(part, slice(k, k + CHUNK))
            depth = slice(part * half + k, part * half + k + CHUNK)
            gate_act += jnp.dot(x, gate_ref[depth, :], preferred_element_type=jnp.float32)
            up_act += jnp.dot(x, up_ref[depth, :], preferred_element_type=jnp.float32)
    hidden = (gate_act / (1.0 + jnp.exp(-gate_act)) * up_act).astype(jnp.bfloat16)
    for part, kept, sent in ((0, keep_a, send_a), (1, keep_b, send_b)):
        copies[4 + part].wait()
        for c in range(0, half, CHUNK):
            cols = slice(part * half + c, part * half + c + CHUNK)
            partial = jnp.dot(hidden, down_ref[:, cols], preferred_element_type=jnp.float32)
            partial = (partial * share).astype(jnp.bfloat16)
            kept[:, c : c + CHUNK] = partial[: rows // 2]
            sent[:, c : c + CHUNK] = partial[rows // 2 :]


def experts(a_all, b_all, picks, expert, w_gate, w_up, w_down):
    rows, half = a_all[0].shape
    out = jax.ShapeDtypeStruct((2 * rows, half), jnp.bfloat16)
    vmem = pl.BlockSpec(memory_space=pltpu.VMEM)
    anywhere = pl.BlockSpec(memory_space=pl.ANY)
    return pl.pallas_call(
        lambda *refs: experts_kernel(picks, *refs),
        out_shape=(out,) * 4,
        in_specs=[pl.BlockSpec(memory_space=pltpu.SMEM)] + [vmem] * 8 + [anywhere] * 3,
        out_specs=[vmem] * 4,
        scratch_shapes=[
            pltpu.VMEM(w_gate.shape, w_gate.dtype),
            pltpu.VMEM(w_up.shape, w_up.dtype),
            pltpu.VMEM(w_down.shape, w_down.dtype),
            pltpu.SemaphoreType.DMA((6,)),
        ],
        compiler_params=pltpu.CompilerParams(vmem_limit_bytes=48 << 20),
        name="experts",
    )(expert.reshape(1), *a_all, *b_all, w_gate, w_up, w_down)


def experts_wide(a_all, b_all, picks, expert, w_gate, w_up, w_down):
    size, half = a_all[0].shape
    size //= 2
    b_all = [
        v
        for early, late in (b_all[:2], b_all[2:])
        for v in (early[:size], late[:size], early[size:], late[size:])
    ]
    a, b = jnp.concatenate(a_all, axis=0), jnp.concatenate(b_all, axis=0)
    info = b[:, half:].astype(jnp.float32)
    scores = info[:, picks : 2 * picks]
    named = jnp.where(info[:, :picks] == expert.astype(jnp.float32), scores, 0.0)
    share = jnp.sum(named, axis=1, keepdims=True) / jnp.sum(scores, axis=1, keepdims=True)
    x = jnp.concatenate([a, b[:, :half]], axis=1)
    gate_act = jnp.dot(x, w_gate, preferred_element_type=jnp.float32)
    up_act = jnp.dot(x, w_up, preferred_element_type=jnp.float32)
    hidden = (jax.nn.silu(gate_act) * up_act).astype(jnp.bfloat16)
    partial = jnp.dot(hidden, w_down, preferred_element_type=jnp.float32)
    partial = (share * partial).astype(jnp.bfloat16)
    rows = 4 * size
    return partial[:rows, :half], partial[:rows, half:], partial[rows:, :half], partial[rows:, half:]


def scatter_rows(keep_a, keep_b, send_a, send_b, slices, cache):
    rows = keep_a.shape[0] // 2
    quarter = rows // 2
    a, b = total(keep_a, swap(send_a, 0)), total(keep_b, swap(send_b, 0))
    a_in = swap(a[rows:], "sec")
    b_in = swap(jnp.concatenate([b[quarter:rows], b[rows + quarter :]], axis=0), 1)
    a_in, b_in, slices, cache = lax.optimization_barrier((a_in, b_in, slices, cache))
    a = total(a[:rows], a_in)
    b = total(jnp.concatenate([b[:quarter], b[rows : rows + quarter]], axis=0), b_in)
    a_in, b_in = swap(a[quarter:], 1), swap(b[quarter:], "sec")
    a, b = total(a[:quarter], a_in), total(b[:quarter], b_in)
    rows = quarter // 2
    a, b = (total(v[:rows], swap(v[rows:], 2)) for v in (a, b))
    return a, b, slices, cache


def latent_kernel(place_ref, kept_ref, in_ref, group_ref, gain_ref, *refs):
    w_refs = refs[:8]
    sums_ref, sums_out, moe_ref, piece_ref = refs[8:]
    rows, half = in_ref.shape
    own = rows // 2
    piece, lat = w_refs[0].shape
    upper = place_ref[0] == 1
    group = jnp.where(upper, group_ref[:, half:], group_ref[:, :half]).astype(jnp.float32)
    received = pltpu.roll(in_ref[...].astype(jnp.float32), own, 0)
    moe = (group + (kept_ref[...] + received)).astype(jnp.bfloat16)
    moe_ref[...] = moe[:own]
    widened = moe.astype(jnp.float32)
    scaled = widened * gain_ref[pl.ds(place_ref[0], 1), :]
    for p in range(8):
        piece_ref[p] = scaled[:, p * piece : (p + 1) * piece]
    sums = jnp.zeros((rows, lat), jnp.float32)
    for slot, w_ref in enumerate(w_refs):
        flips = ((slot & 1) << 1) | ((slot & 2) << 1) | (slot >> 2)
        x = piece_ref[place_ref[1] ^ flips].astype(jnp.bfloat16)
        sums += jnp.dot(x, w_ref[...], preferred_element_type=jnp.float32)
    squares = jnp.sum(widened * widened, axis=1, keepdims=True)
    tail = jnp.broadcast_to(squares, (rows, LANES))
    for ref, first in ((sums_ref, 0), (sums_out, own)):
        ref[:, :lat] = sums[first : first + own]
        ref[:, lat:] = tail[first : first + own, : ref.shape[1] - lat]


def latent_parts(place, kept, received, group, gain, slices):
    rows, half = received.shape
    piece, lat = slices[0].shape
    own = rows // 2
    vmem = pl.BlockSpec(memory_space=pltpu.VMEM)
    padded = -(-(lat + 1) // LANES) * LANES
    sums = jax.ShapeDtypeStruct((own, padded), jnp.float32)
    moe = jax.ShapeDtypeStruct((own, half), jnp.bfloat16)
    return pl.pallas_call(
        latent_kernel,
        out_shape=(sums, sums, moe),
        in_specs=[pl.BlockSpec(memory_space=pltpu.SMEM)] + [vmem] * 12,
        out_specs=[vmem] * 3,
        scratch_shapes=[pltpu.VMEM((8, rows, piece), jnp.float32)],
        compiler_params=pltpu.CompilerParams(vmem_limit_bytes=12 << 20),
        name="latent_parts",
    )(place, kept, received, group, gain.reshape(2, half), *slices)


def moe_kernel(place_ref, mine_ref, extra_ref, sum_ref, group_ref, moe_ref):
    own, half = mine_ref.shape
    upper = place_ref[0] == 1
    group = jnp.where(upper, group_ref[:, :half], group_ref[:, half:])
    other = (sum_ref[...].astype(jnp.float32) + group.astype(jnp.float32))[:own]
    other = (other + extra_ref[...].astype(jnp.float32)).astype(jnp.bfloat16)
    mine = mine_ref[...]
    moe_ref[:, :half] = jnp.where(upper, other, mine)
    moe_ref[:, half:] = jnp.where(upper, mine, other)


def moe_rows(place, mine, extra, other, group):
    own, half = mine.shape
    vmem = pl.BlockSpec(memory_space=pltpu.VMEM)
    return pl.pallas_call(
        moe_kernel,
        out_shape=jax.ShapeDtypeStruct((own, 2 * half), jnp.bfloat16),
        in_specs=[pl.BlockSpec(memory_space=pltpu.SMEM)] + [vmem] * 4,
        out_specs=vmem,
        compiler_params=pltpu.CompilerParams(vmem_limit_bytes=4 << 20),
        name="moe_rows",
    )(place, mine, extra, other, group)


def latent_parts_wide(device, high, mixture, residual, own_rows, norm_gain, slices):
    for bit in reversed(high[:-1]):
        part = mixture.shape[1] // 2
        upper = ((device >> bit) & 1) == 1
        lo, hi = mixture[:, :part], mixture[:, part:]
        sent = flipped(jnp.where(upper, lo, hi), own_rows << (high[-1] - bit))
        mixture = total(jnp.where(upper, hi, lo), swap(sent, bit))
        residual = jnp.where(upper, residual[:, part:], residual[:, :part])
    part = mixture.shape[1]
    moe = (residual.astype(jnp.float32) + mixture.astype(jnp.float32)).astype(jnp.bfloat16)
    widened = moe.astype(jnp.float32)
    gain = lax.dynamic_slice_in_dim(norm_gain, (device >> 3) * part, part, axis=0)
    squares = jnp.sum(widened * widened, axis=1, keepdims=True)
    scaled = (widened * gain).astype(jnp.bfloat16)
    slices = jnp.stack(slices)
    piece = slices.shape[1]
    latent = jnp.zeros((moe.shape[0], slices.shape[2]), jnp.float32)
    for p in range(8):
        flips = (device & 7) ^ p
        slot = ((flips >> 1) & 1) | ((flips >> 1) & 2) | ((flips & 1) << 2)
        weight = lax.dynamic_index_in_dim(slices, slot, axis=0, keepdims=False)
        latent += jnp.dot(
            scaled[:, p * piece : (p + 1) * piece], weight, preferred_element_type=jnp.float32
        )
    sums = jnp.concatenate([latent, squares], axis=1)
    for bit in high:
        rows = sums.shape[0] // 2
        sums = sums[:rows] + swap(sums[rows:], bit)
    for bit in high:
        rows = moe.shape[0] // 2
        upper = ((device >> bit) & 1) == 1
        kept, received = moe[:rows], swap(moe[rows:], bit)
        moe = jnp.where(
            upper,
            jnp.concatenate([received, kept], axis=1),
            jnp.concatenate([kept, received], axis=1),
        )
    return sums, moe


def per_device(
    hidden_in,
    expert_ids,
    gate_scores,
    w_gate,
    w_up,
    w_down,
    norm_gain,
    w_kv,
    queries,
    kv_cache,
    lengths,
):
    devices = lax.axis_size("dev")
    device = lax.axis_index("dev")
    shard_count = FF // w_gate.shape[1]
    expert = lax.axis_index("sec") * (devices // shard_count) + device // shard_count
    high = range(3, devices.bit_length() - 1)
    own_rows, width = hidden_in.shape

    picks = expert_ids.shape[1]
    half = width // 2

    cache = cache_part(queries, kv_cache, lengths)
    group, a_all, b_all, slices = gather_rows(hidden_in, expert_ids, gate_scores, high, w_kv)
    run = experts if len(high) == 1 else experts_wide
    partial = run(a_all, b_all, picks, expert, w_gate, w_up, w_down)
    partial, early = lax.optimization_barrier((partial, slices[:3]))
    a, b, late, (stats, combined) = scatter_rows(*partial, slices[3], cache)
    slices = (*early, late)
    slices += tuple(swap(v, 0) for v in slices)

    upper = (device >> high[-1]) & 1
    if len(high) == 1:
        place = jnp.stack([upper, device & 7])
        kept, other = jnp.where(upper == 1, b, a), jnp.where(upper == 1, a, b)
        received, extra = swap(other, high[0]), swap(kept[own_rows:], high[0])
        pair = jnp.concatenate(group, axis=1)
        sums, sums_out, mine = latent_parts(
            place, kept.astype(jnp.float32), received, pair, norm_gain, slices
        )
        sums_in = swap(sums_out, high[0])
        moe = moe_rows(place, mine, extra, other, pair)
    else:
        mixture = total(jnp.where(upper == 1, b, a), swap(flipped(jnp.where(upper == 1, a, b), own_rows), high[-1]))
        residual = jnp.where(upper == 1, group[1], group[0])
        sums, moe = latent_parts_wide(device, high, mixture, residual, own_rows, norm_gain, slices)
        sums = jnp.pad(sums, ((0, 0), (0, -sums.shape[1] % LANES)))
        sums_in = jnp.zeros_like(sums)
    new_latent, attended = finish(width, sums, sums_in, queries, stats, combined)
    return (moe, new_latent, attended)


def solution(mesh):
    in_specs = (
        P(("sec", "dev"), None),
        P(("sec", "dev"), None),
        P(("sec", "dev"), None),
        P(None, ("sec", "dev")),
        P(None, ("sec", "dev")),
        P(("sec", "dev"), None),
        P(),
        P("dev", None),
        P(("sec", "dev"), None, None),
        P(("sec", "dev"), None, None),
        P(("sec", "dev")),
    )
    out_specs = (P(("sec", "dev"), None), P(("sec", "dev"), None), P(("sec", "dev"), None, None))
    return jax.shard_map(
        per_device, mesh=mesh, in_specs=in_specs, out_specs=out_specs, check_vma=False
    )
```

```python
import jax
import jax.numpy as jnp
from jax import lax
from jax.experimental import pallas as pl
from jax.experimental.pallas import tpu as pltpu
from jax.sharding import PartitionSpec as P

FF = 2048
KV = 512
LANES = 128
CHUNK = 512
CORE, LOW, MID, HIGH = 0, 1, 2, 3


score_scale = 192.0 ** (-0.5)
norm_eps = 1e-06


def swap(x, *bits):
    if bits == ("sec",):
        return lax.ppermute(x, "sec", [(i, i ^ 1) for i in range(lax.axis_size("sec"))])
    flips = sum(1 << bit for bit in bits)
    return lax.ppermute(x, "dev", [(i, i ^ flips) for i in range(lax.axis_size("dev"))])


def wide_total(*parts):
    return sum(part.astype(jnp.float32) for part in parts)


def total(*parts):
    return wide_total(*parts).astype(jnp.bfloat16)


def cache_kernel(lengths_ref, q_ref, kv_ref, stats_ref, out_ref):
    heads, count = q_ref.shape[1], kv_ref.shape[2]
    lane = lax.broadcasted_iota(jnp.int32, (heads, LANES), 1)
    position = lax.broadcasted_iota(jnp.int32, (heads, count), 1)
    for row in range(q_ref.shape[0]):
        scores = jnp.dot(q_ref[row], kv_ref[row], preferred_element_type=jnp.float32) * score_scale
        scores = jnp.where(position < lengths_ref[row], scores, -1e30)
        peak = jnp.max(scores, axis=1, keepdims=True)
        spread = jnp.exp(scores - peak)
        denominator = jnp.sum(spread, axis=1, keepdims=True)
        out_ref[row] = lax.dot_general(
            spread.astype(jnp.bfloat16),
            kv_ref[row, :KV, :],
            (((1,), (1,)), ((), ())),
            preferred_element_type=jnp.float32,
        )
        stats_ref[row] = jnp.where(lane == 0, peak, denominator)


def cache_part(queries, kv_cache, lengths):
    rows, heads = queries.shape[:2]
    vmem = pl.BlockSpec(memory_space=pltpu.VMEM)
    return pl.pallas_call(
        cache_kernel,
        out_shape=(
            jax.ShapeDtypeStruct((rows, heads, LANES), jnp.float32),
            jax.ShapeDtypeStruct((rows, heads, KV), jnp.float32),
        ),
        in_specs=[pl.BlockSpec(memory_space=pltpu.SMEM), vmem, vmem],
        out_specs=[vmem] * 2,
        compiler_params=pltpu.CompilerParams(vmem_limit_bytes=8 << 20),
        cost_estimate=pl.CostEstimate(
            flops=4 * queries.size * kv_cache.shape[1],
            bytes_accessed=2 * kv_cache.size,
            transcendentals=0,
        ),
        name="cache_part",
    )(lengths, queries, jnp.swapaxes(kv_cache, 1, 2))


def kernel_call(body, out_shape, scalars, *arrays, name, mib, anywhere=0, scratch=()):
    vmem = pl.BlockSpec(memory_space=pltpu.VMEM)
    specs = [pl.BlockSpec(memory_space=pltpu.SMEM)] + [vmem] * (len(arrays) - anywhere)
    specs += [pl.BlockSpec(memory_space=pl.ANY)] * anywhere
    return pl.pallas_call(
        body,
        out_shape=out_shape,
        in_specs=specs,
        out_specs=jax.tree.map(lambda _: vmem, out_shape),
        scratch_shapes=scratch,
        compiler_params=pltpu.CompilerParams(vmem_limit_bytes=mib << 20),
        name=name,
    )(scalars, *arrays)


def info_kernel(_, x_ref, ids_ref, scores_ref, out_ref):
    (rows, width), picks = x_ref.shape, ids_ref.shape[0]
    out_ref[:, :width] = x_ref[...]
    lane = lax.broadcasted_iota(jnp.int32, (rows, LANES), 1)
    row = lax.broadcasted_iota(jnp.int32, (rows, rows), 0)
    here = row == lax.broadcasted_iota(jnp.int32, (rows, rows), 1)
    info = jnp.zeros((rows, LANES), jnp.float32)
    for i, values in enumerate((ids_ref[...], scores_ref[...])):
        values = values.astype(jnp.float32)
        for k in range(picks):
            column = jnp.sum(jnp.where(here, values[k : k + 1], 0.0), axis=1, keepdims=True)
            info = jnp.where(lane == i * picks + k, column, info)
    out_ref[:, width:] = info.astype(out_ref.dtype)


def with_info(hidden_in, expert_ids, gate_scores):
    rows, width = hidden_in.shape
    return kernel_call(
        info_kernel,
        jax.ShapeDtypeStruct((rows, width + LANES), hidden_in.dtype),
        jnp.zeros((1,), jnp.int32),
        hidden_in,
        expert_ids.T,
        gate_scores.T,
        name="with_info",
        mib=2,
    )


def pack_kernel(_, *refs):
    blocks, (a_ref, b_ref) = refs[:4], refs[4:]
    half = a_ref.shape[1]
    for ref, cols in ((a_ref, slice(0, half)), (b_ref, slice(half, None))):
        x = jnp.concatenate([block[:, cols].astype(jnp.float32) for block in blocks], axis=0)
        ref[...] = x.astype(ref.dtype)


def pack_rows_of(*blocks):
    rows, width = blocks[0].shape
    half = (width - LANES) // 2
    outs = [jax.ShapeDtypeStruct((4 * rows, cols), jnp.bfloat16) for cols in (half, half + LANES)]
    return kernel_call(
        pack_kernel, tuple(outs), jnp.zeros((1,), jnp.int32), *blocks, name="pack_rows", mib=4
    )


def gather_rows(hidden_in, expert_ids, gate_scores, w_kv):
    x = with_info(hidden_in, expert_ids, gate_scores)
    a, b = pack_rows_of(x, swap(x, HIGH), swap(x, MID), swap(x, MID, HIGH))
    a, b, w_own = lax.optimization_barrier((a, b, w_kv))
    w_mid = swap(w_own, MID)
    a_low, b_sec = swap(a, LOW), swap(b, "sec")
    a, b = jnp.concatenate([a, a_low], axis=0), jnp.concatenate([b, b_sec], axis=0)
    a_all, b_all = (a, swap(a, "sec")), (b, swap(b, LOW))
    a_all += tuple(swap(v, CORE) for v in a_all)
    b_all += tuple(swap(v, CORE) for v in b_all)
    return a_all, b_all, w_mid


def experts_kernel(picks, place_ref, *refs):
    a_refs, b_refs, w_refs, outs = refs[:4], refs[4:8], refs[8:11], refs[11:15]
    gate_ref, up_ref, down_ref, sems = refs[15:]
    size, half = a_refs[0].shape
    size //= 2
    moves = []
    for part in (pl.ds(0, half), pl.ds(half, half)):
        moves.append((w_refs[0].at[part], gate_ref.at[part]))
        moves.append((w_refs[1].at[part], up_ref.at[part]))
    for part in (pl.ds(0, half), pl.ds(half, half)):
        moves.append((w_refs[2].at[:, part], down_ref.at[:, part]))
    copies = [pltpu.make_async_copy(*move, sems.at[i]) for i, move in enumerate(moves)]
    for copy in copies:
        copy.start()

    def rows_of(part, cols):
        if part == 0:
            return jnp.concatenate([ref[:, cols] for ref in a_refs], axis=0)
        blocks = []
        for side in range(2):
            early, late = b_refs[2 * side][:, cols], b_refs[2 * side + 1][:, cols]
            blocks += [early[:size], late[:size], early[size:], late[size:]]
        return jnp.concatenate(blocks, axis=0)

    def ordered(x):
        n = size // 2
        parts = [x[i * n : (i + 1) * n] for i in range(x.shape[0] // n)]
        parts = [jnp.where(place_ref[2] == 1, pltpu.roll(v, n // 2, 0), v) for v in parts]
        done = []
        for i in range(0, len(parts), 4):
            for mid in range(2):
                pair = parts[i + mid], parts[i + 2 + mid]
                done.append(jnp.where(place_ref[1] == 1, pair[1], pair[0]))
                done.append(jnp.where(place_ref[1] == 1, pair[0], pair[1]))
        return jnp.concatenate(done, axis=0)

    info = rows_of(1, slice(half, half + LANES)).astype(jnp.float32)
    rows, hid = info.shape[0], gate_ref.shape[1]
    lane = lax.broadcasted_iota(jnp.int32, info.shape, 1)
    scores = jnp.where(lane < picks, pltpu.roll(info, LANES - picks, 1), 0.0)
    named = jnp.where(info == place_ref[0].astype(jnp.float32), scores, 0.0)
    share = jnp.sum(named, axis=1, keepdims=True) / jnp.sum(scores, axis=1, keepdims=True)
    gate_act = jnp.zeros((rows, hid), jnp.float32)
    up_act = jnp.zeros((rows, hid), jnp.float32)
    for part in range(2):
        copies[2 * part].wait()
        copies[2 * part + 1].wait()
        for k in range(0, half, CHUNK):
            x = rows_of(part, slice(k, k + CHUNK))
            depth = slice(part * half + k, part * half + k + CHUNK)
            gate_act += jnp.dot(x, gate_ref[depth, :], preferred_element_type=jnp.float32)
            up_act += jnp.dot(x, up_ref[depth, :], preferred_element_type=jnp.float32)
    hidden = ordered(gate_act / (1.0 + jnp.exp(-gate_act)) * up_act).astype(jnp.bfloat16)
    share = ordered(jnp.broadcast_to(share, (rows, LANES)))[:, :1]
    copies[4].wait()
    copies[5].wait()
    block = half // 4
    for part in range(2):
        kept, sent = outs[2 * part : 2 * part + 2]
        for i in range(4):
            flip, mid = i // 2, i % 2
            first = (place_ref[2] ^ part) * half + mid * 2 * block + (place_ref[1] ^ flip) * block
            for c in range(0, block, CHUNK):
                wide = min(CHUNK, block - c)
                cols = pl.ds(pl.multiple_of(first + c, LANES), wide)
                partial = jnp.dot(hidden, down_ref[:, cols], preferred_element_type=jnp.float32)
                partial = (partial * share).astype(jnp.bfloat16)
                to = slice(i * block + c, i * block + c + wide)
                kept[:, to] = partial[: rows // 2]
                sent[:, to] = partial[rows // 2 :]


def experts(place, a_all, b_all, picks, w_gate, w_up, w_down):
    rows, half = a_all[0].shape
    out = jax.ShapeDtypeStruct((2 * rows, half), jnp.bfloat16)
    weights = (w_gate, w_up, w_down)
    return kernel_call(
        lambda *refs: experts_kernel(picks, *refs),
        (out,) * 4,
        place,
        *a_all,
        *b_all,
        *weights,
        name="experts",
        mib=48,
        anywhere=3,
        scratch=[pltpu.VMEM(w.shape, w.dtype) for w in weights] + [pltpu.SemaphoreType.DMA((6,))],
    )


def scatter_rows(keep_a, send_a, keep_b, send_b, late):
    rows, cols = keep_a.shape[0] // 2, keep_a.shape[1] // 2
    left, right = slice(0, cols), slice(cols, None)
    a, b = [keep_a, swap(send_a, CORE)], [keep_b, swap(send_b, CORE)]
    a.append(swap(total(*(v[rows:] for v in a)), "sec"))
    b.append(swap(total(*(v[:, right] for v in b)), LOW))
    a, b, late = lax.optimization_barrier((a, b, late))
    a.append(swap(total(*(v[:rows, right] for v in a)), LOW))
    b.append(swap(total(*(v[rows:, left] for v in b)), "sec"))
    a, b = lax.optimization_barrier((a, b))
    rows //= 2
    here, there = slice(0, rows), slice(rows, 2 * rows)
    ins = (
        swap(total(*(v[there, left] for v in a)), MID),
        swap(total(*(v[here, left] for v in b)), HIGH),
        swap(total(*(v[there, left] for v in b)), MID, HIGH),
    )
    a, ins = lax.optimization_barrier((a, ins))
    return wide_total(*(v[here, left] for v in a)), ins, late


def residual_kernel(place_ref, a_ref, b_ref, low_ref, out_ref):
    rows, half = a_ref.shape
    n, block = rows // 4, half // 4
    upper, odd = place_ref[2] == 1, place_ref[1] == 1
    pair = []
    for a, b in ((a_ref[:n], b_ref[:n]), (a_ref[2 * n : 3 * n], low_ref[:n])):
        x = jnp.where(upper, b[:, :half].astype(jnp.float32), a.astype(jnp.float32))
        pair.append(jnp.where(upper, pltpu.roll(x, n // 2, 0), x))
    pair = [jnp.where(odd, pair[1], pair[0]), jnp.where(odd, pair[0], pair[1])]
    x = jnp.concatenate(pair, axis=0)
    for mid in range(2):
        first = 2 * mid * block
        even = x[:, first : first + block]
        out_ref[:, mid * block : (mid + 1) * block] = jnp.where(
            odd, x[:, first + block : first + 2 * block], even
        )


def residual_rows(place, a, b, b_low):
    rows, half = a.shape
    return kernel_call(
        residual_kernel,
        jax.ShapeDtypeStruct((rows // 2, half // 2), jnp.float32),
        place,
        a,
        b,
        b_low,
        name="residual_rows",
        mib=4,
    )


def put_split(ref, first, apart, x):
    cols = x.shape[1]
    upper = x.astype(jnp.bfloat16)
    ref[:, first : first + cols] = upper
    rest = (x - upper.astype(jnp.float32)).astype(jnp.bfloat16)
    ref[:, first + apart : first + apart + cols] = rest


def get_split(ref, first, cols):
    upper = ref[:, first : first + cols].astype(jnp.float32)
    return upper + ref[:, first + cols : first + 2 * cols].astype(jnp.float32)


def latent_kernel(place_ref, sum_ref, residual_ref, gain_ref, *refs):
    in_refs, w_refs = refs[:3], refs[3:7]
    sums_ref, moe_ref, out_ref, piece_ref = refs[7:]
    rows, cols = sum_ref.shape
    block, n = cols // 2, rows // 2
    piece, lat = w_refs[0].shape
    odd = place_ref[1] == 1
    mixture = sum_ref[...] + wide_total(*(ref[...] for ref in in_refs))
    moe = (residual_ref[...] + mixture).astype(jnp.bfloat16)
    widened = moe.astype(jnp.float32)
    moe_ref[...] = jnp.where(odd, widened[n:], widened[:n]).astype(jnp.bfloat16)
    out_ref[:, :cols] = jnp.where(odd, widened[:n], widened[n:]).astype(jnp.bfloat16)
    for mid in range(2):
        gain = gain_ref[pl.ds(4 * place_ref[2] + 2 * mid + place_ref[1], 1), :]
        scaled = widened[:, mid * block : (mid + 1) * block] * gain
        for core in range(2):
            piece_ref[2 * mid + core] = scaled[:, core * piece : (core + 1) * piece]
    sums = jnp.zeros((rows, lat), jnp.float32)
    for flips, w_ref in enumerate(w_refs):
        x = piece_ref[place_ref[3] ^ flips].astype(jnp.bfloat16)
        sums += jnp.dot(x, w_ref[...], preferred_element_type=jnp.float32)
    squares = jnp.sum(widened * widened, axis=1, keepdims=True)
    tail = jnp.broadcast_to(squares, (rows, LANES))
    wide = sums_ref.shape[1]
    for to, x in ((slice(0, lat), sums), (slice(lat, wide), tail[:, : wide - lat])):
        sums_ref[:, to] = jnp.where(odd, x[n:], x[:n])
        put_split(out_ref, cols + to.start, wide, jnp.where(odd, x[:n], x[n:]))


def latent_parts(place, kept, received, residual, gain, slices):
    rows, cols = kept.shape
    piece, lat = slices[0].shape
    padded = -(-(lat + 1) // LANES) * LANES
    sums = jax.ShapeDtypeStruct((rows // 2, padded), jnp.float32)
    moe = jax.ShapeDtypeStruct((rows // 2, cols), jnp.bfloat16)
    sent = jax.ShapeDtypeStruct((rows // 2, cols + 2 * padded), jnp.bfloat16)
    return kernel_call(
        latent_kernel,
        (sums, moe, sent),
        place,
        kept,
        residual,
        gain.reshape(8, cols // 2),
        *received,
        *slices,
        name="latent_parts",
        mib=12,
        scratch=[pltpu.VMEM((4, rows, piece), jnp.float32)],
    )


def turn_kernel(place_ref, sums_ref, moe_ref, in_ref, sums_out, moe_out, send_ref):
    rows, cols = moe_ref.shape
    n, wide = rows // 2, sums_ref.shape[1]
    upper = place_ref[2] == 1
    sums = sums_ref[...] + get_split(in_ref, cols, wide)
    sums_out[...] = jnp.where(upper, sums[n:], sums[:n])
    put_split(send_ref, 2 * cols, wide, jnp.where(upper, sums[:n], sums[n:]))
    for first, x in ((0, moe_ref[...]), (cols, in_ref[:, :cols])):
        x = x.astype(jnp.float32)
        to = slice(first, first + cols)
        moe_out[:, to] = jnp.where(upper, x[n:], x[:n]).astype(jnp.bfloat16)
        send_ref[:, to] = jnp.where(upper, x[:n], x[n:]).astype(jnp.bfloat16)


def turn(place, sums, moe, received):
    (rows, cols), wide = moe.shape, sums.shape[1]
    return kernel_call(
        turn_kernel,
        (
            jax.ShapeDtypeStruct((rows // 2, wide), sums.dtype),
            jax.ShapeDtypeStruct((rows // 2, 2 * cols), moe.dtype),
            jax.ShapeDtypeStruct((rows // 2, 2 * cols + 2 * wide), moe.dtype),
        ),
        place,
        sums,
        moe,
        received,
        name="turn",
        mib=2,
    )


def put_rows(place_ref, keep_ref, in_ref, out_ref):
    half = keep_ref.shape[1]
    block = half // 4
    upper, odd = place_ref[2] == 1, place_ref[1] == 1
    for part, ref, other in ((0, keep_ref, in_ref), (1, in_ref, keep_ref)):
        x = jnp.where(upper, other[:, :half], ref[:, :half])
        for mid in range(2):
            even = x[:, mid * block : (mid + 1) * block]
            uneven = x[:, (2 + mid) * block : (3 + mid) * block]
            first = part * half + mid * 2 * block
            out_ref[:, first : first + block] = jnp.where(odd, uneven, even)
            out_ref[:, first + block : first + 2 * block] = jnp.where(odd, even, uneven)


def finish_kernel(place_ref, sums_ref, moe_ref, in_ref, q_ref, stats_ref, part_ref, *outs):
    moe_out, latent_ref, out_ref = outs
    lat, half = q_ref.shape[2], moe_ref.shape[1]
    sums = sums_ref[...] + get_split(in_ref, half, sums_ref.shape[1])
    inverse = lax.rsqrt(sums[:, lat : lat + 1] / (2 * half) + norm_eps)
    rounded = (sums[:, :lat] * inverse).astype(jnp.bfloat16)
    latent_ref[...] = rounded
    latent = rounded.astype(jnp.float32)
    for row in range(q_ref.shape[0]):
        own = latent[row : row + 1]
        own_score = jnp.sum(q_ref[row].astype(jnp.float32) * own, axis=1, keepdims=True) * score_scale
        peak, denominator = stats_ref[row, :, 0:1], stats_ref[row, :, 1:2]
        top = jnp.maximum(peak, own_score)
        shrink = jnp.exp(peak - top)
        own_weight = jnp.exp(own_score - top)
        scale = 1.0 / (denominator * shrink + own_weight)
        own_prob = (own_weight * scale).astype(jnp.bfloat16).astype(jnp.float32)
        value = part_ref[row] * (shrink * scale) + own_prob * own[:, :KV]
        out_ref[row] = value.astype(jnp.bfloat16)
    put_rows(place_ref, moe_ref, in_ref, moe_out)


def finish(place, sums, moe, received, queries, stats, combined):
    rows, heads, lat = queries.shape
    outs = ((rows, 2 * moe.shape[1]), (rows, lat), (rows, heads, KV))
    return kernel_call(
        finish_kernel,
        tuple(jax.ShapeDtypeStruct(shape, jnp.bfloat16) for shape in outs),
        place,
        sums,
        moe,
        received,
        queries,
        stats,
        combined,
        name="finish",
        mib=8,
    )


def per_device(
    hidden_in,
    expert_ids,
    gate_scores,
    w_gate,
    w_up,
    w_down,
    norm_gain,
    w_kv,
    queries,
    kv_cache,
    lengths,
):
    devices = lax.axis_size("dev")
    device = lax.axis_index("dev")
    shard_count = FF // w_gate.shape[1]
    expert = lax.axis_index("sec") * (devices // shard_count) + device // shard_count
    picks = expert_ids.shape[1]
    core_mid = (((device >> MID) & 1) << 1) | (device & 1)
    place = jnp.stack([expert, (device >> LOW) & 1, (device >> HIGH) & 1, core_mid])

    cache = cache_part(queries, kv_cache, lengths)
    a_all, b_all, w_mid = gather_rows(hidden_in, expert_ids, gate_scores, w_kv)
    partial = experts(place, a_all, b_all, picks, w_gate, w_up, w_down)
    partial, w_mid = lax.optimization_barrier((partial, w_mid))
    kept, received, (stats, combined) = scatter_rows(*partial, cache)
    slices = (w_kv, swap(w_kv, CORE), w_mid, swap(w_mid, CORE))
    residual = residual_rows(place, a_all[0], b_all[0], b_all[1])
    sums, moe, sent = latent_parts(place, kept, received, residual, norm_gain, slices)
    sums, moe, sent = turn(place, sums, moe, swap(sent, LOW))
    return finish(place, sums, moe, swap(sent, HIGH), queries, stats, combined)


def shifted(x, axis, by):
    length = lax.axis_size(axis)
    return lax.ppermute(x, axis, [(i, (i + by) % length) for i in range(length)])


def attend(queries, kv_cache, lengths, latent_new, value_width):
    length_max = kv_cache.shape[1]
    scores = (
        jnp.einsum("bhl,bpl->bhp", queries, kv_cache, preferred_element_type=jnp.float32)
        * score_scale
    )
    visible = jnp.arange(length_max, dtype=jnp.int32)[None, None, :] < lengths[:, None, None]
    scores = jnp.where(visible, scores, -1e30)
    own_score = (
        jnp.einsum("bhl,bl->bh", queries, latent_new, preferred_element_type=jnp.float32)
        * score_scale
    )
    peak = jnp.maximum(jnp.max(scores, axis=2), own_score)
    spread = jnp.exp(scores - peak[:, :, None])
    own_weight = jnp.exp(own_score - peak)
    denominator = jnp.sum(spread, axis=2) + own_weight
    cache_weights = (spread / denominator[:, :, None]).astype(jnp.bfloat16)
    own_prob = (own_weight / denominator).astype(jnp.bfloat16)
    values = kv_cache[:, :, :value_width]
    combined = jnp.einsum("bhp,bpv->bhv", cache_weights, values, preferred_element_type=jnp.float32)
    combined = combined + own_prob.astype(jnp.float32)[:, :, None] * latent_new[
        :, None, :value_width
    ].astype(jnp.float32)
    return combined.astype(jnp.bfloat16)


def route_tables(expert_ids, gate_scores, section, per_section, total_experts, capacity):
    row_count, pick_count = expert_ids.shape
    weights = gate_scores.astype(jnp.float32)
    weights = weights / jnp.sum(weights, axis=1, keepdims=True)
    flat_ids = expert_ids.reshape(-1)
    onehot = (flat_ids[:, None] == jnp.arange(total_experts, dtype=jnp.int32)[None, :]).astype(
        jnp.int32
    )
    before = jnp.cumsum(onehot, axis=0) - onehot
    position = jnp.sum(before * onehot, axis=1)
    local_ids = flat_ids - section * per_section
    matches = (
        local_ids[None, None, :] == jnp.arange(per_section, dtype=jnp.int32)[:, None, None]
    ) & (position[None, None, :] == jnp.arange(capacity, dtype=jnp.int32)[None, :, None])
    matches = matches.reshape(per_section, capacity, row_count, pick_count)
    members = jnp.sum(matches.astype(jnp.float32), axis=3).astype(jnp.bfloat16)
    shares = jnp.sum(jnp.where(matches, weights[None, None], 0.0), axis=3)
    return (members, shares)


def pack_rows(members, rows_in, shard_count):
    per_section, capacity = (members.shape[0], members.shape[1])
    packed = jnp.einsum("ecb,bd->ecd", members, rows_in, preferred_element_type=jnp.float32).astype(
        jnp.bfloat16
    )
    widened = jnp.broadcast_to(
        packed[:, None], (per_section, shard_count, capacity, rows_in.shape[1])
    )
    return widened.reshape(per_section * shard_count, capacity, rows_in.shape[1])


def unpack(returned, shares, shard_count):
    per_section, capacity = (shares.shape[0], shares.shape[1])
    summed = jnp.sum(
        returned.astype(jnp.float32).reshape(per_section, shard_count, capacity, returned.shape[2]),
        axis=1,
    )
    return jnp.einsum("ecb,ecd->bd", shares, summed, precision=lax.Precision.HIGHEST)


def run_expert(slots, w_gate, w_up, w_down):
    flat_rows = slots.reshape(-1, slots.shape[-1])
    gate_act = jnp.dot(flat_rows, w_gate, preferred_element_type=jnp.float32)
    up_act = jnp.dot(flat_rows, w_up, preferred_element_type=jnp.float32)
    hidden = (jax.nn.silu(gate_act) * up_act).astype(jnp.bfloat16)
    partial_value = jnp.dot(hidden, w_down, preferred_element_type=jnp.float32).astype(jnp.bfloat16)
    return partial_value.reshape(slots.shape)


def per_device_wide(
    hidden_in,
    expert_ids,
    gate_scores,
    w_gate,
    w_up,
    w_down,
    norm_gain,
    w_kv,
    queries,
    kv_cache,
    lengths,
):
    sections = lax.axis_size("sec")
    devices = lax.axis_size("dev")
    section = lax.axis_index("sec")
    shard_count = FF // w_gate.shape[1]
    per_section = devices // shard_count
    total_experts = sections * per_section
    row_count, pick_count = expert_ids.shape
    capacity = max(2, (2 * row_count * pick_count + total_experts - 1) // total_experts)
    tables = [
        route_tables(
            expert_ids,
            gate_scores,
            (section + offset) % sections,
            per_section,
            total_experts,
            capacity,
        )
        for offset in range(2)
    ]
    outgoing = jnp.stack(
        [pack_rows(tables[offset][0], hidden_in, shard_count) for offset in range(2)]
    )
    incoming = lax.all_to_all(outgoing, "dev", split_axis=1, concat_axis=1, tiled=True)
    crossed = shifted(incoming[1], "sec", 1)
    local_slots = jnp.stack([incoming[0], crossed])
    results = run_expert(local_slots, w_gate, w_up, w_down)
    returned = shifted(results[1], "sec", 1)
    sending = jnp.stack([results[0], returned])
    back = lax.all_to_all(sending, "dev", split_axis=1, concat_axis=1, tiled=True)
    mixture = unpack(back[0], tables[0][1], shard_count) + unpack(
        back[1], tables[1][1], shard_count
    )
    moe_out = (hidden_in.astype(jnp.float32) + mixture).astype(jnp.bfloat16)
    widened = moe_out.astype(jnp.float32)
    normed = (
        widened
        * lax.rsqrt(jnp.mean(widened * widened, axis=1, keepdims=True) + norm_eps)
        * norm_gain
    ).astype(jnp.bfloat16)
    pieces = lax.all_to_all(normed, "dev", split_axis=1, concat_axis=0, tiled=True)
    latent_sum = lax.psum_scatter(
        jnp.dot(pieces, w_kv, preferred_element_type=jnp.float32),
        "dev",
        scatter_dimension=0,
        tiled=True,
    )
    new_latent = latent_sum.astype(jnp.bfloat16)
    attended = attend(queries, kv_cache, lengths, new_latent, KV)
    return (moe_out, new_latent, attended)


def solution(mesh):
    in_specs = (
        P(("sec", "dev"), None),
        P(("sec", "dev"), None),
        P(("sec", "dev"), None),
        P(None, ("sec", "dev")),
        P(None, ("sec", "dev")),
        P(("sec", "dev"), None),
        P(),
        P("dev", None),
        P(("sec", "dev"), None, None),
        P(("sec", "dev"), None, None),
        P(("sec", "dev")),
    )
    out_specs = (P(("sec", "dev"), None), P(("sec", "dev"), None), P(("sec", "dev"), None, None))
    pairwise = mesh.shape["sec"] == 2 and mesh.shape["dev"] == 2 << HIGH
    return jax.shard_map(
        per_device if pairwise else per_device_wide, mesh=mesh, in_specs=in_specs, out_specs=out_specs, check_vma=False
    )
```

```python
import jax
import jax.numpy as jnp
from jax import lax
from jax.experimental import pallas as pl
from jax.experimental.pallas import tpu as pltpu
from jax.sharding import PartitionSpec as P

FF = 2048
KV = 512
LANES = 128
CHUNK = 512
COLS = 896
CORE, LOW, MID, HIGH = 0, 1, 2, 3


score_scale = 192.0 ** (-0.5)
norm_eps = 1e-06


def swap(x, *bits):
    if bits == ("sec",):
        return lax.ppermute(x, "sec", [(i, i ^ 1) for i in range(lax.axis_size("sec"))])
    flips = sum(1 << bit for bit in bits)
    return lax.ppermute(x, "dev", [(i, i ^ flips) for i in range(lax.axis_size("dev"))])


def swap_both(x, bit):
    size = lax.axis_size("dev")
    pairs = [(i, i ^ (1 << bit) ^ size) for i in range(2 * size)]
    return lax.ppermute(x, ("sec", "dev"), pairs)


def wide_total(*parts):
    return sum(part.astype(jnp.float32) for part in parts)


def total(*parts):
    return wide_total(*parts).astype(jnp.bfloat16)


def cache_kernel(lengths_ref, q_ref, kv_ref, stats_ref, out_ref):
    heads, count = q_ref.shape[1], kv_ref.shape[2]
    lane = lax.broadcasted_iota(jnp.int32, (heads, LANES), 1)
    position = lax.broadcasted_iota(jnp.int32, (heads, count), 1)
    for row in range(q_ref.shape[0]):
        scores = jnp.dot(q_ref[row], kv_ref[row], preferred_element_type=jnp.float32) * score_scale
        scores = jnp.where(position < lengths_ref[row], scores, -1e30)
        peak = jnp.max(scores, axis=1, keepdims=True)
        spread = jnp.exp(scores - peak)
        denominator = jnp.sum(spread, axis=1, keepdims=True)
        out_ref[row] = lax.dot_general(
            spread.astype(jnp.bfloat16),
            kv_ref[row, :KV, :],
            (((1,), (1,)), ((), ())),
            preferred_element_type=jnp.float32,
        )
        stats_ref[row] = jnp.where(lane == 0, peak, denominator)


def cache_part(queries, kv_cache, lengths):
    rows, heads = queries.shape[:2]
    vmem = pl.BlockSpec(memory_space=pltpu.VMEM)
    return pl.pallas_call(
        cache_kernel,
        out_shape=(
            jax.ShapeDtypeStruct((rows, heads, LANES), jnp.float32),
            jax.ShapeDtypeStruct((rows, heads, KV), jnp.float32),
        ),
        in_specs=[pl.BlockSpec(memory_space=pltpu.SMEM), vmem, vmem],
        out_specs=[vmem] * 2,
        compiler_params=pltpu.CompilerParams(vmem_limit_bytes=8 << 20),
        cost_estimate=pl.CostEstimate(
            flops=4 * queries.size * kv_cache.shape[1],
            bytes_accessed=2 * kv_cache.size,
            transcendentals=0,
        ),
        name="cache_part",
    )(lengths, queries, jnp.swapaxes(kv_cache, 1, 2))


def kernel_call(body, out_shape, scalars, *arrays, name, mib, anywhere=0, scratch=()):
    vmem = pl.BlockSpec(memory_space=pltpu.VMEM)
    specs = [pl.BlockSpec(memory_space=pltpu.SMEM)] + [vmem] * (len(arrays) - anywhere)
    specs += [pl.BlockSpec(memory_space=pl.ANY)] * anywhere
    return pl.pallas_call(
        body,
        out_shape=out_shape,
        in_specs=specs,
        out_specs=jax.tree.map(lambda _: vmem, out_shape),
        scratch_shapes=scratch,
        compiler_params=pltpu.CompilerParams(vmem_limit_bytes=mib << 20),
        name=name,
    )(scalars, *arrays)


def with_info(hidden_in, expert_ids, gate_scores):
    width, picks = hidden_in.shape[1], expert_ids.shape[1]
    x = jnp.pad(hidden_in, ((0, 0), (0, LANES)))
    column = lax.broadcasted_iota(jnp.int32, x.shape, 1) - width
    for i, values in enumerate((expert_ids.astype(x.dtype), gate_scores)):
        for k in range(picks):
            x = jnp.where(column == i * picks + k, values[:, k : k + 1], x)
    return x


def pack_kernel(_, *refs):
    blocks, (a_ref, b_ref) = refs[:4], refs[4:]
    half = a_ref.shape[1]
    for ref, cols in ((a_ref, slice(0, half)), (b_ref, slice(half, None))):
        x = jnp.concatenate([block[:, cols].astype(jnp.float32) for block in blocks], axis=0)
        ref[...] = x.astype(ref.dtype)


def pack_rows_of(*blocks):
    rows, width = blocks[0].shape
    half = (width - LANES) // 2
    outs = [jax.ShapeDtypeStruct((4 * rows, cols), jnp.bfloat16) for cols in (half, half + LANES)]
    return kernel_call(
        pack_kernel, tuple(outs), jnp.zeros((1,), jnp.int32), *blocks, name="pack_rows", mib=4
    )


def gather_rows(hidden_in, expert_ids, gate_scores, w_kv):
    x = with_info(hidden_in, expert_ids, gate_scores)
    a, b = pack_rows_of(x, swap(x, HIGH), swap(x, MID), swap(x, MID, HIGH))
    a, b, w_own = lax.optimization_barrier((a, b, w_kv))
    w_mid = swap(w_own, MID)
    a_low, b_sec = swap(a, LOW), swap(b, "sec")
    a, b = jnp.concatenate([a, a_low], axis=0), jnp.concatenate([b, b_sec], axis=0)
    a_all, b_all = (a, swap(a, "sec")), (b, swap(b, LOW))
    a_all += tuple(swap(v, CORE) for v in a_all)
    b_all += tuple(swap(v, CORE) for v in b_all)
    return a_all, b_all, w_mid


def experts_kernel(picks, place_ref, *refs):
    a_refs, b_refs, w_refs, outs = refs[:4], refs[4:8], refs[8:11], refs[11:15]
    gate_ref, up_ref, down_ref, sems = refs[15:]
    size, half = a_refs[0].shape
    size //= 2
    moves = []
    for part in (pl.ds(0, half), pl.ds(half, half)):
        moves.append((w_refs[0].at[part], gate_ref.at[part]))
        moves.append((w_refs[1].at[part], up_ref.at[part]))
    for flip in range(2):
        part = pl.ds(pl.multiple_of((place_ref[2] ^ flip) * half, LANES), half)
        moves.append((w_refs[2].at[:, part], down_ref.at[:, part]))
    copies = [pltpu.make_async_copy(*move, sems.at[i]) for i, move in enumerate(moves)]
    for copy in copies:
        copy.start()

    def rows_of(part, cols):
        if part == 0:
            return jnp.concatenate([ref[:, cols] for ref in a_refs], axis=0)
        blocks = []
        for side in range(2):
            early, late = b_refs[2 * side][:, cols], b_refs[2 * side + 1][:, cols]
            blocks += [early[:size], late[:size], early[size:], late[size:]]
        return jnp.concatenate(blocks, axis=0)

    def ordered(x):
        n = size // 2
        parts = [x[i * n : (i + 1) * n] for i in range(x.shape[0] // n)]
        parts = [jnp.where(place_ref[2] == 1, pltpu.roll(v, n // 2, 0), v) for v in parts]
        done = []
        for i in range(0, len(parts), 4):
            for mid in range(2):
                pair = parts[i + mid], parts[i + 2 + mid]
                done.append(jnp.where(place_ref[1] == 1, pair[1], pair[0]))
                done.append(jnp.where(place_ref[1] == 1, pair[0], pair[1]))
        return jnp.concatenate(done, axis=0)

    info = rows_of(1, slice(half, half + LANES)).astype(jnp.float32)
    rows, hid = info.shape[0], gate_ref.shape[1]
    lane = lax.broadcasted_iota(jnp.int32, info.shape, 1)
    scores = jnp.where(lane < picks, pltpu.roll(info, LANES - picks, 1), 0.0)
    named = jnp.where(info == place_ref[0].astype(jnp.float32), scores, 0.0)
    share = jnp.sum(named, axis=1, keepdims=True) / jnp.sum(scores, axis=1, keepdims=True)
    gate_act = jnp.zeros((rows, hid), jnp.float32)
    up_act = jnp.zeros((rows, hid), jnp.float32)
    for part in range(2):
        copies[2 * part].wait()
        copies[2 * part + 1].wait()
        for k in range(0, half, CHUNK):
            x = rows_of(part, slice(k, k + CHUNK))
            depth = slice(part * half + k, part * half + k + CHUNK)
            gate_act += jnp.dot(x, gate_ref[depth, :], preferred_element_type=jnp.float32)
            up_act += jnp.dot(x, up_ref[depth, :], preferred_element_type=jnp.float32)
    hidden = ordered(gate_act / (1.0 + jnp.exp(-gate_act)) * up_act).astype(jnp.bfloat16)
    share = ordered(jnp.broadcast_to(share, (rows, LANES)))[:, :1]
    block = half // 4
    for flip in range(2):
        copies[4 + flip].wait()
        for j in range(4):
            part, mid = j // 2, j % 2
            i = 2 * flip + mid
            kept, sent = outs[2 * part : 2 * part + 2]
            first = (place_ref[2] ^ flip) * half + mid * 2 * block + (place_ref[1] ^ part) * block
            for c in range(0, block, COLS):
                wide = min(COLS, block - c)
                cols = pl.ds(pl.multiple_of(first + c, LANES), wide)
                partial = jnp.dot(hidden, down_ref[:, cols], preferred_element_type=jnp.float32)
                partial = (partial * share).astype(jnp.bfloat16)
                to = slice(i * block + c, i * block + c + wide)
                kept[:, to] = partial[: rows // 2]
                sent[:, to] = partial[rows // 2 :]


def experts(place, a_all, b_all, picks, w_gate, w_up, w_down):
    rows, half = a_all[0].shape
    out = jax.ShapeDtypeStruct((2 * rows, half), jnp.bfloat16)
    weights = (w_gate, w_up, w_down)
    return kernel_call(
        lambda *refs: experts_kernel(picks, *refs),
        (out,) * 4,
        place,
        *a_all,
        *b_all,
        *weights,
        name="experts",
        mib=48,
        anywhere=3,
        scratch=[pltpu.VMEM(w.shape, w.dtype) for w in weights] + [pltpu.SemaphoreType.DMA((6,))],
    )


def scatter_rows(keep_a, send_a, keep_b, send_b, late):
    rows, cols = keep_a.shape[0] // 2, keep_a.shape[1] // 2
    here, there, left, right = slice(0, rows), slice(rows, None), slice(0, cols), slice(cols, None)
    b = [keep_b, swap(send_b, CORE)]
    a = [keep_a, swap(send_a, CORE)]
    ins = [
        swap(total(*(v[here] for v in b)), LOW),
        swap(total(*(v[there] for v in a)), "sec"),
        swap_both(total(*(v[there] for v in b)), LOW),
    ]
    a, ins, late = lax.optimization_barrier((a, ins, late))
    a += ins
    rows //= 2
    here, there = slice(0, rows), slice(rows, 2 * rows)
    ins = (
        swap(total(*(v[here, right] for v in a)), HIGH),
        swap(total(*(v[there, right] for v in a)), MID, HIGH),
        swap(total(*(v[there, left] for v in a)), MID),
    )
    a, ins = lax.optimization_barrier((a, ins))
    return wide_total(*(v[here, left] for v in a)), ins, late


def residual_kernel(place_ref, a_ref, b_ref, low_ref, out_ref):
    rows, half = a_ref.shape
    n, block = rows // 4, half // 4
    upper, odd = place_ref[2] == 1, place_ref[1] == 1
    pair = []
    for a, b in ((a_ref[:n], b_ref[:n]), (a_ref[2 * n : 3 * n], low_ref[:n])):
        x = jnp.where(upper, b[:, :half].astype(jnp.float32), a.astype(jnp.float32))
        pair.append(jnp.where(upper, pltpu.roll(x, n // 2, 0), x))
    pair = [jnp.where(odd, pair[1], pair[0]), jnp.where(odd, pair[0], pair[1])]
    x = jnp.concatenate(pair, axis=0)
    for mid in range(2):
        first = 2 * mid * block
        even = x[:, first : first + block]
        out_ref[:, mid * block : (mid + 1) * block] = jnp.where(
            odd, x[:, first + block : first + 2 * block], even
        )


def residual_rows(place, a, b, b_low):
    rows, half = a.shape
    return kernel_call(
        residual_kernel,
        jax.ShapeDtypeStruct((rows // 2, half // 2), jnp.float32),
        place,
        a,
        b,
        b_low,
        name="residual_rows",
        mib=4,
    )


OTHERS = ((1, 0), (0, 1), (1, 1))


def put_split(ref, first, apart, x):
    cols = x.shape[1]
    upper = x.astype(jnp.bfloat16)
    ref[:, first : first + cols] = upper
    rest = (x - upper.astype(jnp.float32)).astype(jnp.bfloat16)
    ref[:, first + apart : first + apart + cols] = rest


def get_split(ref, first, cols):
    upper = ref[:, first : first + cols].astype(jnp.float32)
    return upper + ref[:, first + cols : first + 2 * cols].astype(jnp.float32)


def latent_kernel(place_ref, sum_ref, residual_ref, gain_ref, *refs):
    in_refs, w_refs = refs[:3], refs[3:7]
    sums_ref, moe_ref, piece_ref = refs[7], refs[8], refs[12]
    rows, cols = sum_ref.shape
    block, n = cols // 2, rows // 4
    piece, lat = w_refs[0].shape


    def rows_for(x, low, high):
        x = jnp.where(place_ref[1] == 1 - low, x[2 * n :], x[: 2 * n])
        return jnp.where(place_ref[2] == 1 - high, x[n:], x[:n])

    mixture = sum_ref[...] + wide_total(*(ref[...] for ref in in_refs))
    moe = (residual_ref[...] + mixture).astype(jnp.bfloat16)
    widened = moe.astype(jnp.float32)
    for mid in range(2):
        gain = gain_ref[pl.ds(4 * place_ref[2] + 2 * mid + place_ref[1], 1), :]
        scaled = widened[:, mid * block : (mid + 1) * block] * gain
        for core in range(2):
            piece_ref[2 * mid + core] = scaled[:, core * piece : (core + 1) * piece]
    sums = jnp.zeros((rows, lat), jnp.float32)
    for flips, w_ref in enumerate(w_refs):
        x = piece_ref[place_ref[3] ^ flips].astype(jnp.bfloat16)
        sums += jnp.dot(x, w_ref[...], preferred_element_type=jnp.float32)
    squares = jnp.sum(widened * widened, axis=1, keepdims=True)
    tail = jnp.broadcast_to(squares, (rows, LANES))
    wide = sums_ref.shape[1]
    tail = tail[:, : wide - lat]
    moe_ref[...] = rows_for(widened, 0, 0).astype(jnp.bfloat16)
    sums_ref[:, :lat] = rows_for(sums, 0, 0)
    sums_ref[:, lat:] = rows_for(tail, 0, 0)
    for (low, high), ref in zip(OTHERS, refs[9:12]):
        ref[:, :cols] = rows_for(widened, low, high).astype(jnp.bfloat16)
        put_split(ref, cols, wide, rows_for(sums, low, high))
        put_split(ref, cols + lat, wide, rows_for(tail, low, high))


def latent_parts(place, kept, received, residual, gain, slices):
    rows, cols = kept.shape
    piece, lat = slices[0].shape
    padded = -(-(lat + 1) // LANES) * LANES
    sums = jax.ShapeDtypeStruct((rows // 4, padded), jnp.float32)
    moe = jax.ShapeDtypeStruct((rows // 4, cols), jnp.bfloat16)
    sent = jax.ShapeDtypeStruct((rows // 4, cols + 2 * padded), jnp.bfloat16)
    return kernel_call(
        latent_kernel,
        (sums, moe, sent, sent, sent),
        place,
        kept,
        residual,
        gain,
        *received,
        *slices,
        name="latent_parts",
        mib=32,
        scratch=[pltpu.VMEM((4, rows, piece), jnp.float32)],
    )


def put_rows(place_ref, blocks, out_ref):
    cols = blocks[0][0].shape[1]
    block = cols // 2
    for high in range(2):
        parts = [jnp.where(place_ref[2] == high, x[0], x[1]) for x in blocks]
        for low in range(2):
            x = jnp.where(place_ref[1] == low, parts[0], parts[1])
            for mid in range(2):
                first = 2 * high * cols + mid * cols + low * block
                out_ref[:, first : first + block] = x[:, mid * block : (mid + 1) * block]


def finish_kernel(place_ref, sums_ref, moe_ref, q_ref, stats_ref, part_ref, *refs):
    in_refs, (moe_out, latent_ref, out_ref) = refs[:3], refs[3:]
    lat, cols = q_ref.shape[2], moe_ref.shape[1]
    sums = sums_ref[...]
    for ref in in_refs:
        sums += get_split(ref, cols, sums_ref.shape[1])
    inverse = lax.rsqrt(sums[:, lat : lat + 1] / (4 * cols) + norm_eps)
    rounded = (sums[:, :lat] * inverse).astype(jnp.bfloat16)
    latent_ref[...] = rounded
    latent = rounded.astype(jnp.float32)
    for row in range(q_ref.shape[0]):
        own = latent[row : row + 1]
        own_score = jnp.sum(q_ref[row].astype(jnp.float32) * own, axis=1, keepdims=True) * score_scale
        peak, denominator = stats_ref[row, :, 0:1], stats_ref[row, :, 1:2]
        top = jnp.maximum(peak, own_score)
        shrink = jnp.exp(peak - top)
        own_weight = jnp.exp(own_score - top)
        scale = 1.0 / (denominator * shrink + own_weight)
        own_prob = (own_weight * scale).astype(jnp.bfloat16).astype(jnp.float32)
        value = part_ref[row] * (shrink * scale) + own_prob * own[:, :KV]
        out_ref[row] = value.astype(jnp.bfloat16)
    other_low, other_high, other_both = (ref[:, :cols] for ref in in_refs)
    put_rows(place_ref, ((moe_ref[...], other_high), (other_low, other_both)), moe_out)


def finish(place, sums, moe, received, queries, stats, combined):
    rows, heads, lat = queries.shape
    outs = ((rows, 4 * moe.shape[1]), (rows, lat), (rows, heads, KV))
    return kernel_call(
        finish_kernel,
        tuple(jax.ShapeDtypeStruct(shape, jnp.bfloat16) for shape in outs),
        place,
        sums,
        moe,
        queries,
        stats,
        combined,
        *received,
        name="finish",
        mib=8,
    )


def per_device(
    hidden_in,
    expert_ids,
    gate_scores,
    w_gate,
    w_up,
    w_down,
    norm_gain,
    w_kv,
    queries,
    kv_cache,
    lengths,
):
    devices = lax.axis_size("dev")
    device = lax.axis_index("dev")
    shard_count = FF // w_gate.shape[1]
    expert = lax.axis_index("sec") * (devices // shard_count) + device // shard_count
    picks = expert_ids.shape[1]
    core_mid = (((device >> MID) & 1) << 1) | (device & 1)
    place = jnp.stack([expert, (device >> LOW) & 1, (device >> HIGH) & 1, core_mid])

    cache = cache_part(queries, kv_cache, lengths)
    a_all, b_all, w_mid = gather_rows(hidden_in, expert_ids, gate_scores, w_kv)
    partial = experts(place, a_all, b_all, picks, w_gate, w_up, w_down)
    partial, w_mid = lax.optimization_barrier((partial, w_mid))
    kept, received, late = scatter_rows(*partial, (cache,))
    (cache,) = late
    stats, combined = cache
    residual = residual_rows(place, a_all[0], b_all[0], b_all[1])
    gain = norm_gain.reshape(8, -1)
    slices = (w_kv, swap(w_kv, CORE), w_mid, swap(w_mid, CORE))
    sums, moe, *sent = latent_parts(place, kept, received, residual, gain, slices)
    bits = ((LOW,), (HIGH,), (LOW, HIGH))
    received = {i: swap(sent[i], *bits[i]) for i in (1, 2, 0)}
    received = [received[i] for i in range(3)]
    return finish(place, sums, moe, received, queries, stats, combined)


def shifted(x, axis, by):
    length = lax.axis_size(axis)
    return lax.ppermute(x, axis, [(i, (i + by) % length) for i in range(length)])


def attend(queries, kv_cache, lengths, latent_new, value_width):
    length_max = kv_cache.shape[1]
    scores = (
        jnp.einsum("bhl,bpl->bhp", queries, kv_cache, preferred_element_type=jnp.float32)
        * score_scale
    )
    visible = jnp.arange(length_max, dtype=jnp.int32)[None, None, :] < lengths[:, None, None]
    scores = jnp.where(visible, scores, -1e30)
    own_score = (
        jnp.einsum("bhl,bl->bh", queries, latent_new, preferred_element_type=jnp.float32)
        * score_scale
    )
    peak = jnp.maximum(jnp.max(scores, axis=2), own_score)
    spread = jnp.exp(scores - peak[:, :, None])
    own_weight = jnp.exp(own_score - peak)
    denominator = jnp.sum(spread, axis=2) + own_weight
    cache_weights = (spread / denominator[:, :, None]).astype(jnp.bfloat16)
    own_prob = (own_weight / denominator).astype(jnp.bfloat16)
    values = kv_cache[:, :, :value_width]
    combined = jnp.einsum("bhp,bpv->bhv", cache_weights, values, preferred_element_type=jnp.float32)
    combined = combined + own_prob.astype(jnp.float32)[:, :, None] * latent_new[
        :, None, :value_width
    ].astype(jnp.float32)
    return combined.astype(jnp.bfloat16)


def route_tables(expert_ids, gate_scores, section, per_section, total_experts, capacity):
    row_count, pick_count = expert_ids.shape
    weights = gate_scores.astype(jnp.float32)
    weights = weights / jnp.sum(weights, axis=1, keepdims=True)
    flat_ids = expert_ids.reshape(-1)
    onehot = (flat_ids[:, None] == jnp.arange(total_experts, dtype=jnp.int32)[None, :]).astype(
        jnp.int32
    )
    before = jnp.cumsum(onehot, axis=0) - onehot
    position = jnp.sum(before * onehot, axis=1)
    local_ids = flat_ids - section * per_section
    matches = (
        local_ids[None, None, :] == jnp.arange(per_section, dtype=jnp.int32)[:, None, None]
    ) & (position[None, None, :] == jnp.arange(capacity, dtype=jnp.int32)[None, :, None])
    matches = matches.reshape(per_section, capacity, row_count, pick_count)
    members = jnp.sum(matches.astype(jnp.float32), axis=3).astype(jnp.bfloat16)
    shares = jnp.sum(jnp.where(matches, weights[None, None], 0.0), axis=3)
    return (members, shares)


def pack_rows(members, rows_in, shard_count):
    per_section, capacity = (members.shape[0], members.shape[1])
    packed = jnp.einsum("ecb,bd->ecd", members, rows_in, preferred_element_type=jnp.float32).astype(
        jnp.bfloat16
    )
    widened = jnp.broadcast_to(
        packed[:, None], (per_section, shard_count, capacity, rows_in.shape[1])
    )
    return widened.reshape(per_section * shard_count, capacity, rows_in.shape[1])


def unpack(returned, shares, shard_count):
    per_section, capacity = (shares.shape[0], shares.shape[1])
    summed = jnp.sum(
        returned.astype(jnp.float32).reshape(per_section, shard_count, capacity, returned.shape[2]),
        axis=1,
    )
    return jnp.einsum("ecb,ecd->bd", shares, summed, precision=lax.Precision.HIGHEST)


def run_expert(slots, w_gate, w_up, w_down):
    flat_rows = slots.reshape(-1, slots.shape[-1])
    gate_act = jnp.dot(flat_rows, w_gate, preferred_element_type=jnp.float32)
    up_act = jnp.dot(flat_rows, w_up, preferred_element_type=jnp.float32)
    hidden = (jax.nn.silu(gate_act) * up_act).astype(jnp.bfloat16)
    partial_value = jnp.dot(hidden, w_down, preferred_element_type=jnp.float32).astype(jnp.bfloat16)
    return partial_value.reshape(slots.shape)


def per_device_wide(
    hidden_in,
    expert_ids,
    gate_scores,
    w_gate,
    w_up,
    w_down,
    norm_gain,
    w_kv,
    queries,
    kv_cache,
    lengths,
):
    sections = lax.axis_size("sec")
    devices = lax.axis_size("dev")
    section = lax.axis_index("sec")
    shard_count = FF // w_gate.shape[1]
    per_section = devices // shard_count
    total_experts = sections * per_section
    row_count, pick_count = expert_ids.shape
    capacity = max(2, (2 * row_count * pick_count + total_experts - 1) // total_experts)
    tables = [
        route_tables(
            expert_ids,
            gate_scores,
            (section + offset) % sections,
            per_section,
            total_experts,
            capacity,
        )
        for offset in range(2)
    ]
    outgoing = jnp.stack(
        [pack_rows(tables[offset][0], hidden_in, shard_count) for offset in range(2)]
    )
    incoming = lax.all_to_all(outgoing, "dev", split_axis=1, concat_axis=1, tiled=True)
    crossed = shifted(incoming[1], "sec", 1)
    local_slots = jnp.stack([incoming[0], crossed])
    results = run_expert(local_slots, w_gate, w_up, w_down)
    returned = shifted(results[1], "sec", 1)
    sending = jnp.stack([results[0], returned])
    back = lax.all_to_all(sending, "dev", split_axis=1, concat_axis=1, tiled=True)
    mixture = unpack(back[0], tables[0][1], shard_count) + unpack(
        back[1], tables[1][1], shard_count
    )
    moe_out = (hidden_in.astype(jnp.float32) + mixture).astype(jnp.bfloat16)
    widened = moe_out.astype(jnp.float32)
    normed = (
        widened
        * lax.rsqrt(jnp.mean(widened * widened, axis=1, keepdims=True) + norm_eps)
        * norm_gain
    ).astype(jnp.bfloat16)
    pieces = lax.all_to_all(normed, "dev", split_axis=1, concat_axis=0, tiled=True)
    latent_sum = lax.psum_scatter(
        jnp.dot(pieces, w_kv, preferred_element_type=jnp.float32),
        "dev",
        scatter_dimension=0,
        tiled=True,
    )
    new_latent = latent_sum.astype(jnp.bfloat16)
    attended = attend(queries, kv_cache, lengths, new_latent, KV)
    return (moe_out, new_latent, attended)


def solution(mesh):
    in_specs = (
        P(("sec", "dev"), None),
        P(("sec", "dev"), None),
        P(("sec", "dev"), None),
        P(None, ("sec", "dev")),
        P(None, ("sec", "dev")),
        P(("sec", "dev"), None),
        P(),
        P("dev", None),
        P(("sec", "dev"), None, None),
        P(("sec", "dev"), None, None),
        P(("sec", "dev")),
    )
    out_specs = (P(("sec", "dev"), None), P(("sec", "dev"), None), P(("sec", "dev"), None, None))
    pairwise = mesh.shape["sec"] == 2 and mesh.shape["dev"] == 2 << HIGH
    return jax.shard_map(
        per_device if pairwise else per_device_wide, mesh=mesh, in_specs=in_specs, out_specs=out_specs, check_vma=False
    )
```

```python
import jax
import jax.numpy as jnp
from jax import lax
from jax.experimental import pallas as pl
from jax.experimental.pallas import tpu as pltpu
from jax.sharding import PartitionSpec as P

FF = 2048
KV = 512
LANES = 128
CHUNK = 512
COLS = 896
CORE, LOW, MID, HIGH = 0, 1, 2, 3


score_scale = 192.0 ** (-0.5)
norm_eps = 1e-06


def swap(x, *bits):
    if bits == ("sec",):
        return lax.ppermute(x, "sec", [(i, i ^ 1) for i in range(lax.axis_size("sec"))])
    flips = sum(1 << bit for bit in bits)
    return lax.ppermute(x, "dev", [(i, i ^ flips) for i in range(lax.axis_size("dev"))])


def swap_both(x, bit):
    size = lax.axis_size("dev")
    pairs = [(i, i ^ (1 << bit) ^ size) for i in range(2 * size)]
    return lax.ppermute(x, ("sec", "dev"), pairs)


def wide_total(*parts):
    return sum(part.astype(jnp.float32) for part in parts)


def total(*parts):
    return wide_total(*parts).astype(jnp.bfloat16)


def cache_kernel(lengths_ref, q_ref, kv_ref, stats_ref, out_ref):
    heads, count = q_ref.shape[1], kv_ref.shape[2]
    lane = lax.broadcasted_iota(jnp.int32, (heads, LANES), 1)
    position = lax.broadcasted_iota(jnp.int32, (heads, count), 1)
    for row in range(q_ref.shape[0]):
        scores = jnp.dot(q_ref[row], kv_ref[row], preferred_element_type=jnp.float32) * score_scale
        scores = jnp.where(position < lengths_ref[row], scores, -1e30)
        peak = jnp.max(scores, axis=1, keepdims=True)
        spread = jnp.exp(scores - peak)
        denominator = jnp.sum(spread, axis=1, keepdims=True)
        out_ref[row] = lax.dot_general(
            spread.astype(jnp.bfloat16),
            kv_ref[row, :KV, :],
            (((1,), (1,)), ((), ())),
            preferred_element_type=jnp.float32,
        )
        stats_ref[row] = jnp.where(lane == 0, peak, denominator)


def cache_part(queries, kv_cache, lengths):
    rows, heads = queries.shape[:2]
    vmem = pl.BlockSpec(memory_space=pltpu.VMEM)
    return pl.pallas_call(
        cache_kernel,
        out_shape=(
            jax.ShapeDtypeStruct((rows, heads, LANES), jnp.float32),
            jax.ShapeDtypeStruct((rows, heads, KV), jnp.float32),
        ),
        in_specs=[pl.BlockSpec(memory_space=pltpu.SMEM), vmem, vmem],
        out_specs=[vmem] * 2,
        compiler_params=pltpu.CompilerParams(vmem_limit_bytes=8 << 20),
        cost_estimate=pl.CostEstimate(
            flops=4 * queries.size * kv_cache.shape[1],
            bytes_accessed=2 * kv_cache.size,
            transcendentals=0,
        ),
        name="cache_part",
    )(lengths, queries, jnp.swapaxes(kv_cache, 1, 2))


def kernel_call(body, out_shape, scalars, *arrays, name, mib, anywhere=0, scratch=()):
    vmem = pl.BlockSpec(memory_space=pltpu.VMEM)
    specs = [pl.BlockSpec(memory_space=pltpu.SMEM)] + [vmem] * (len(arrays) - anywhere)
    specs += [pl.BlockSpec(memory_space=pl.ANY)] * anywhere
    return pl.pallas_call(
        body,
        out_shape=out_shape,
        in_specs=specs,
        out_specs=jax.tree.map(lambda _: vmem, out_shape),
        scratch_shapes=scratch,
        compiler_params=pltpu.CompilerParams(vmem_limit_bytes=mib << 20),
        name=name,
    )(scalars, *arrays)


def with_info(hidden_in, expert_ids, gate_scores):
    width, picks = hidden_in.shape[1], expert_ids.shape[1]
    x = jnp.pad(hidden_in, ((0, 0), (0, LANES)))
    column = lax.broadcasted_iota(jnp.int32, x.shape, 1) - width
    for i, values in enumerate((expert_ids.astype(x.dtype), gate_scores)):
        for k in range(picks):
            x = jnp.where(column == i * picks + k, values[:, k : k + 1], x)
    return x


def pack_kernel(_, *refs):
    *blocks, out_ref = refs
    x = jnp.concatenate([block[...].astype(jnp.float32) for block in blocks], axis=0)
    out_ref[...] = x.astype(out_ref.dtype)


def pack_rows_of(*blocks):
    rows, width = blocks[0].shape
    out = jax.ShapeDtypeStruct((len(blocks) * rows, width), blocks[0].dtype)
    return kernel_call(
        pack_kernel, out, jnp.zeros((1,), jnp.int32), *blocks, name="pack_rows", mib=4
    )


def gather_rows(hidden_in, expert_ids, gate_scores, w_kv):
    x = with_info(hidden_in, expert_ids, gate_scores)
    high, mid, both = swap(x, HIGH), swap(x, MID), swap(x, MID, HIGH)
    mid, w_own = lax.optimization_barrier((mid, w_kv))
    x = pack_rows_of(x, high, mid, both)
    blocks = [x, swap(x, LOW), swap(x, "sec"), swap_both(x, LOW)]
    w_mid = swap(w_own, MID)
    return blocks + [swap(v, CORE) for v in blocks], w_mid


def experts_kernel(picks, place_ref, *refs):
    x_refs, w_refs, outs = refs[:8], refs[8:11], refs[11:15]
    gate_ref, up_ref, down_ref, sems = refs[15:]
    size, half = x_refs[0].shape
    half = (half - LANES) // 2
    moves = []
    for part in (pl.ds(0, half), pl.ds(half, half)):
        moves.append((w_refs[0].at[part], gate_ref.at[part]))
        moves.append((w_refs[1].at[part], up_ref.at[part]))
    for flip in range(2):
        part = pl.ds(pl.multiple_of((place_ref[2] ^ flip) * half, LANES), half)
        moves.append((w_refs[2].at[:, part], down_ref.at[:, part]))
    copies = [pltpu.make_async_copy(*move, sems.at[i]) for i, move in enumerate(moves)]
    for copy in copies:
        copy.start()

    def columns(cols):
        return jnp.concatenate([ref[:, cols] for ref in x_refs], axis=0)

    def ordered(x):
        n = size // 2
        parts = [x[i * n : (i + 1) * n] for i in range(x.shape[0] // n)]
        parts = [jnp.where(place_ref[2] == 1, pltpu.roll(v, n // 2, 0), v) for v in parts]
        done = []
        for i in range(0, len(parts), 4):
            for mid in range(2):
                pair = parts[i + mid], parts[i + 2 + mid]
                done.append(jnp.where(place_ref[1] == 1, pair[1], pair[0]))
                done.append(jnp.where(place_ref[1] == 1, pair[0], pair[1]))
        return jnp.concatenate(done, axis=0)

    info = columns(slice(2 * half, None)).astype(jnp.float32)
    rows, hid = info.shape[0], gate_ref.shape[1]
    lane = lax.broadcasted_iota(jnp.int32, info.shape, 1)
    scores = jnp.where(lane < picks, pltpu.roll(info, LANES - picks, 1), 0.0)
    named = jnp.where(info == place_ref[0].astype(jnp.float32), scores, 0.0)
    share = jnp.sum(named, axis=1, keepdims=True) / jnp.sum(scores, axis=1, keepdims=True)
    gate_act = jnp.zeros((rows, hid), jnp.float32)
    up_act = jnp.zeros((rows, hid), jnp.float32)
    for part in range(2):
        copies[2 * part].wait()
        copies[2 * part + 1].wait()
        for k in range(0, half, CHUNK):
            depth = slice(part * half + k, part * half + k + CHUNK)
            x = columns(depth)
            gate_act += jnp.dot(x, gate_ref[depth, :], preferred_element_type=jnp.float32)
            up_act += jnp.dot(x, up_ref[depth, :], preferred_element_type=jnp.float32)
    hidden = ordered(gate_act / (1.0 + jnp.exp(-gate_act)) * up_act).astype(jnp.bfloat16)
    share = ordered(jnp.broadcast_to(share, (rows, LANES)))[:, :1]
    block = half // 4
    for flip in range(2):
        copies[4 + flip].wait()
        for j in range(4):
            part, mid = j // 2, j % 2
            i = 2 * flip + mid
            kept, sent = outs[2 * part : 2 * part + 2]
            first = (place_ref[2] ^ flip) * half + mid * 2 * block + (place_ref[1] ^ part) * block
            for c in range(0, block, COLS):
                wide = min(COLS, block - c)
                cols = pl.ds(pl.multiple_of(first + c, LANES), wide)
                partial = jnp.dot(hidden, down_ref[:, cols], preferred_element_type=jnp.float32)
                partial = (partial * share).astype(jnp.bfloat16)
                to = slice(i * block + c, i * block + c + wide)
                kept[:, to] = partial[: rows // 2]
                sent[:, to] = partial[rows // 2 :]


def experts(place, blocks, picks, w_gate, w_up, w_down):
    out = jax.ShapeDtypeStruct((4 * blocks[0].shape[0], w_gate.shape[0] // 2), jnp.bfloat16)
    weights = (w_gate, w_up, w_down)
    return kernel_call(
        lambda *refs: experts_kernel(picks, *refs),
        (out,) * 4,
        place,
        *blocks,
        *weights,
        name="experts",
        mib=48,
        anywhere=3,
        scratch=[pltpu.VMEM(w.shape, w.dtype) for w in weights] + [pltpu.SemaphoreType.DMA((6,))],
    )


def scatter_rows(keep_a, send_a, keep_b, send_b, late):
    rows, cols = keep_a.shape[0] // 2, keep_a.shape[1] // 2
    here, there, left, right = slice(0, rows), slice(rows, None), slice(0, cols), slice(cols, None)
    b = [keep_b, swap(send_b, CORE)]
    a = [keep_a, swap(send_a, CORE)]
    ins = [
        swap(total(*(v[here] for v in b)), LOW),
        swap(total(*(v[there] for v in a)), "sec"),
        swap_both(total(*(v[there] for v in b)), LOW),
    ]
    a, ins, late = lax.optimization_barrier((a, ins, late))
    a += ins
    rows //= 2
    here, there = slice(0, rows), slice(rows, 2 * rows)
    ins = (
        swap(total(*(v[here, right] for v in a)), HIGH),
        swap(total(*(v[there, right] for v in a)), MID, HIGH),
        swap(total(*(v[there, left] for v in a)), MID),
    )
    return wide_total(*(v[here, left] for v in a)), ins, late


def residual_kernel(place_ref, own_ref, low_ref, out_ref):
    rows, cols = out_ref.shape
    n, block = rows // 2, cols // 2
    upper, odd = place_ref[2] == 1, place_ref[1] == 1
    pair = []
    for ref in (own_ref, low_ref):
        x = ref[:n].astype(jnp.float32)
        x = jnp.where(upper, x[:, 2 * cols : 4 * cols], x[:, : 2 * cols])
        pair.append(jnp.where(upper, pltpu.roll(x, n // 2, 0), x))
    pair = [jnp.where(odd, pair[1], pair[0]), jnp.where(odd, pair[0], pair[1])]
    x = jnp.concatenate(pair, axis=0)
    for mid in range(2):
        first = 2 * mid * block
        even = x[:, first : first + block]
        out_ref[:, mid * block : (mid + 1) * block] = jnp.where(
            odd, x[:, first + block : first + 2 * block], even
        )


def residual_rows(place, own, low):
    rows, width = own.shape
    out = jax.ShapeDtypeStruct((rows, (width - LANES) // 4), jnp.float32)
    return kernel_call(residual_kernel, out, place, own, low, name="residual_rows", mib=4)


OTHERS = ((1, 0), (0, 1), (1, 1))

def put_split(ref, first, apart, x):
    cols = x.shape[1]
    upper = x.astype(jnp.bfloat16)
    ref[:, first : first + cols] = upper
    rest = (x - upper.astype(jnp.float32)).astype(jnp.bfloat16)
    ref[:, first + apart : first + apart + cols] = rest


def get_split(ref, first, cols):
    upper = ref[:, first : first + cols].astype(jnp.float32)
    return upper + ref[:, first + cols : first + 2 * cols].astype(jnp.float32)


def latent_kernel(place_ref, sum_ref, residual_ref, gain_ref, *refs):
    in_refs, w_refs = refs[:3], refs[3:7]
    sums_ref, moe_ref, piece_ref = refs[7], refs[8], refs[12]
    rows, cols = sum_ref.shape
    block, n = cols // 2, rows // 4
    piece, lat = w_refs[0].shape


    def rows_for(x, low, high):
        x = jnp.where(place_ref[1] == 1 - low, x[2 * n :], x[: 2 * n])
        return jnp.where(place_ref[2] == 1 - high, x[n:], x[:n])

    mixture = sum_ref[...] + wide_total(*(ref[...] for ref in in_refs))
    moe = (residual_ref[...] + mixture).astype(jnp.bfloat16)
    widened = moe.astype(jnp.float32)
    for mid in range(2):
        first = (4 * place_ref[2] + 2 * mid + place_ref[1]) * block
        gain = gain_ref[:, pl.ds(pl.multiple_of(first, LANES), block)]
        scaled = widened[:, mid * block : (mid + 1) * block] * gain
        for core in range(2):
            piece_ref[2 * mid + core] = scaled[:, core * piece : (core + 1) * piece]
    sums = jnp.zeros((rows, lat), jnp.float32)
    for flips, w_ref in enumerate(w_refs):
        x = piece_ref[place_ref[3] ^ flips].astype(jnp.bfloat16)
        sums += jnp.dot(x, w_ref[...], preferred_element_type=jnp.float32)
    squares = jnp.sum(widened * widened, axis=1, keepdims=True)
    tail = jnp.broadcast_to(squares, (rows, LANES))
    wide = sums_ref.shape[1]
    tail = tail[:, : wide - lat]
    moe_ref[...] = rows_for(widened, 0, 0).astype(jnp.bfloat16)
    sums_ref[:, :lat] = rows_for(sums, 0, 0)
    sums_ref[:, lat:] = rows_for(tail, 0, 0)
    for (low, high), ref in zip(OTHERS, refs[9:12]):
        ref[:, :cols] = rows_for(widened, low, high).astype(jnp.bfloat16)
        put_split(ref, cols, wide, rows_for(sums, low, high))
        put_split(ref, cols + lat, wide, rows_for(tail, low, high))


def latent_parts(place, kept, received, residual, gain, slices):
    rows, cols = kept.shape
    piece, lat = slices[0].shape
    padded = -(-(lat + 1) // LANES) * LANES
    sums = jax.ShapeDtypeStruct((rows // 4, padded), jnp.float32)
    moe = jax.ShapeDtypeStruct((rows // 4, cols), jnp.bfloat16)
    sent = jax.ShapeDtypeStruct((rows // 4, cols + 2 * padded), jnp.bfloat16)
    return kernel_call(
        latent_kernel,
        (sums, moe, sent, sent, sent),
        place,
        kept,
        residual,
        gain,
        *received,
        *slices,
        name="latent_parts",
        mib=32,
        scratch=[pltpu.VMEM((4, rows, piece), jnp.float32)],
    )


def put_rows(place_ref, blocks, out_ref):
    cols = blocks[0][0].shape[1]
    block = cols // 2
    for high in range(2):
        parts = [jnp.where(place_ref[2] == high, x[0], x[1]) for x in blocks]
        for low in range(2):
            x = jnp.where(place_ref[1] == low, parts[0], parts[1])
            for mid in range(2):
                first = 2 * high * cols + mid * cols + low * block
                out_ref[:, first : first + block] = x[:, mid * block : (mid + 1) * block]


def finish_kernel(place_ref, sums_ref, moe_ref, q_ref, stats_ref, part_ref, *refs):
    in_refs, (moe_out, latent_ref, out_ref) = refs[:3], refs[3:]
    lat, cols = q_ref.shape[2], moe_ref.shape[1]
    sums = sums_ref[...]
    for ref in in_refs:
        sums += get_split(ref, cols, sums_ref.shape[1])
    inverse = lax.rsqrt(sums[:, lat : lat + 1] / (4 * cols) + norm_eps)
    rounded = (sums[:, :lat] * inverse).astype(jnp.bfloat16)
    latent_ref[...] = rounded
    latent = rounded.astype(jnp.float32)
    for row in range(q_ref.shape[0]):
        own = latent[row : row + 1]
        own_score = jnp.sum(q_ref[row].astype(jnp.float32) * own, axis=1, keepdims=True) * score_scale
        peak, denominator = stats_ref[row, :, 0:1], stats_ref[row, :, 1:2]
        top = jnp.maximum(peak, own_score)
        shrink = jnp.exp(peak - top)
        own_weight = jnp.exp(own_score - top)
        scale = 1.0 / (denominator * shrink + own_weight)
        own_prob = (own_weight * scale).astype(jnp.bfloat16).astype(jnp.float32)
        value = part_ref[row] * (shrink * scale) + own_prob * own[:, :KV]
        out_ref[row] = value.astype(jnp.bfloat16)
    other_low, other_high, other_both = (ref[:, :cols] for ref in in_refs)
    put_rows(place_ref, ((moe_ref[...], other_high), (other_low, other_both)), moe_out)


def finish(place, sums, moe, received, queries, stats, combined):
    rows, heads, lat = queries.shape
    outs = ((rows, 4 * moe.shape[1]), (rows, lat), (rows, heads, KV))
    return kernel_call(
        finish_kernel,
        tuple(jax.ShapeDtypeStruct(shape, jnp.bfloat16) for shape in outs),
        place,
        sums,
        moe,
        queries,
        stats,
        combined,
        *received,
        name="finish",
        mib=8,
    )


def per_device(
    hidden_in,
    expert_ids,
    gate_scores,
    w_gate,
    w_up,
    w_down,
    norm_gain,
    w_kv,
    queries,
    kv_cache,
    lengths,
):
    devices = lax.axis_size("dev")
    device = lax.axis_index("dev")
    shard_count = FF // w_gate.shape[1]
    expert = lax.axis_index("sec") * (devices // shard_count) + device // shard_count
    picks = expert_ids.shape[1]
    core_mid = (((device >> MID) & 1) << 1) | (device & 1)
    place = jnp.stack([expert, (device >> LOW) & 1, (device >> HIGH) & 1, core_mid])

    cache = cache_part(queries, kv_cache, lengths)
    blocks, w_mid = gather_rows(hidden_in, expert_ids, gate_scores, w_kv)
    partial = experts(place, blocks, picks, w_gate, w_up, w_down)
    partial, w_mid = lax.optimization_barrier((partial, w_mid))
    kept, received, late = scatter_rows(*partial, (cache,))
    (cache,) = late
    stats, combined = cache
    residual = residual_rows(place, blocks[0], blocks[1])
    gain = norm_gain.reshape(1, -1)
    slices = (w_kv, swap(w_kv, CORE), w_mid, swap(w_mid, CORE))
    sums, moe, *sent = latent_parts(place, kept, received, residual, gain, slices)
    bits = ((LOW,), (HIGH,), (LOW, HIGH))
    received = {i: swap(sent[i], *bits[i]) for i in (1, 2, 0)}
    received = [received[i] for i in range(3)]
    return finish(place, sums, moe, received, queries, stats, combined)


def shifted(x, axis, by):
    length = lax.axis_size(axis)
    return lax.ppermute(x, axis, [(i, (i + by) % length) for i in range(length)])


def attend(queries, kv_cache, lengths, latent_new, value_width):
    length_max = kv_cache.shape[1]
    scores = (
        jnp.einsum("bhl,bpl->bhp", queries, kv_cache, preferred_element_type=jnp.float32)
        * score_scale
    )
    visible = jnp.arange(length_max, dtype=jnp.int32)[None, None, :] < lengths[:, None, None]
    scores = jnp.where(visible, scores, -1e30)
    own_score = (
        jnp.einsum("bhl,bl->bh", queries, latent_new, preferred_element_type=jnp.float32)
        * score_scale
    )
    peak = jnp.maximum(jnp.max(scores, axis=2), own_score)
    spread = jnp.exp(scores - peak[:, :, None])
    own_weight = jnp.exp(own_score - peak)
    denominator = jnp.sum(spread, axis=2) + own_weight
    cache_weights = (spread / denominator[:, :, None]).astype(jnp.bfloat16)
    own_prob = (own_weight / denominator).astype(jnp.bfloat16)
    values = kv_cache[:, :, :value_width]
    combined = jnp.einsum("bhp,bpv->bhv", cache_weights, values, preferred_element_type=jnp.float32)
    combined = combined + own_prob.astype(jnp.float32)[:, :, None] * latent_new[
        :, None, :value_width
    ].astype(jnp.float32)
    return combined.astype(jnp.bfloat16)


def route_tables(expert_ids, gate_scores, section, per_section, total_experts, capacity):
    row_count, pick_count = expert_ids.shape
    weights = gate_scores.astype(jnp.float32)
    weights = weights / jnp.sum(weights, axis=1, keepdims=True)
    flat_ids = expert_ids.reshape(-1)
    onehot = (flat_ids[:, None] == jnp.arange(total_experts, dtype=jnp.int32)[None, :]).astype(
        jnp.int32
    )
    before = jnp.cumsum(onehot, axis=0) - onehot
    position = jnp.sum(before * onehot, axis=1)
    local_ids = flat_ids - section * per_section
    matches = (
        local_ids[None, None, :] == jnp.arange(per_section, dtype=jnp.int32)[:, None, None]
    ) & (position[None, None, :] == jnp.arange(capacity, dtype=jnp.int32)[None, :, None])
    matches = matches.reshape(per_section, capacity, row_count, pick_count)
    members = jnp.sum(matches.astype(jnp.float32), axis=3).astype(jnp.bfloat16)
    shares = jnp.sum(jnp.where(matches, weights[None, None], 0.0), axis=3)
    return (members, shares)


def pack_rows(members, rows_in, shard_count):
    per_section, capacity = (members.shape[0], members.shape[1])
    packed = jnp.einsum("ecb,bd->ecd", members, rows_in, preferred_element_type=jnp.float32).astype(
        jnp.bfloat16
    )
    widened = jnp.broadcast_to(
        packed[:, None], (per_section, shard_count, capacity, rows_in.shape[1])
    )
    return widened.reshape(per_section * shard_count, capacity, rows_in.shape[1])


def unpack(returned, shares, shard_count):
    per_section, capacity = (shares.shape[0], shares.shape[1])
    summed = jnp.sum(
        returned.astype(jnp.float32).reshape(per_section, shard_count, capacity, returned.shape[2]),
        axis=1,
    )
    return jnp.einsum("ecb,ecd->bd", shares, summed, precision=lax.Precision.HIGHEST)


def run_expert(slots, w_gate, w_up, w_down):
    flat_rows = slots.reshape(-1, slots.shape[-1])
    gate_act = jnp.dot(flat_rows, w_gate, preferred_element_type=jnp.float32)
    up_act = jnp.dot(flat_rows, w_up, preferred_element_type=jnp.float32)
    hidden = (jax.nn.silu(gate_act) * up_act).astype(jnp.bfloat16)
    partial_value = jnp.dot(hidden, w_down, preferred_element_type=jnp.float32).astype(jnp.bfloat16)
    return partial_value.reshape(slots.shape)


def per_device_wide(
    hidden_in,
    expert_ids,
    gate_scores,
    w_gate,
    w_up,
    w_down,
    norm_gain,
    w_kv,
    queries,
    kv_cache,
    lengths,
):
    sections = lax.axis_size("sec")
    devices = lax.axis_size("dev")
    section = lax.axis_index("sec")
    shard_count = FF // w_gate.shape[1]
    per_section = devices // shard_count
    total_experts = sections * per_section
    row_count, pick_count = expert_ids.shape
    capacity = max(2, (2 * row_count * pick_count + total_experts - 1) // total_experts)
    tables = [
        route_tables(
            expert_ids,
            gate_scores,
            (section + offset) % sections,
            per_section,
            total_experts,
            capacity,
        )
        for offset in range(2)
    ]
    outgoing = jnp.stack(
        [pack_rows(tables[offset][0], hidden_in, shard_count) for offset in range(2)]
    )
    incoming = lax.all_to_all(outgoing, "dev", split_axis=1, concat_axis=1, tiled=True)
    crossed = shifted(incoming[1], "sec", 1)
    local_slots = jnp.stack([incoming[0], crossed])
    results = run_expert(local_slots, w_gate, w_up, w_down)
    returned = shifted(results[1], "sec", 1)
    sending = jnp.stack([results[0], returned])
    back = lax.all_to_all(sending, "dev", split_axis=1, concat_axis=1, tiled=True)
    mixture = unpack(back[0], tables[0][1], shard_count) + unpack(
        back[1], tables[1][1], shard_count
    )
    moe_out = (hidden_in.astype(jnp.float32) + mixture).astype(jnp.bfloat16)
    widened = moe_out.astype(jnp.float32)
    normed = (
        widened
        * lax.rsqrt(jnp.mean(widened * widened, axis=1, keepdims=True) + norm_eps)
        * norm_gain
    ).astype(jnp.bfloat16)
    pieces = lax.all_to_all(normed, "dev", split_axis=1, concat_axis=0, tiled=True)
    latent_sum = lax.psum_scatter(
        jnp.dot(pieces, w_kv, preferred_element_type=jnp.float32),
        "dev",
        scatter_dimension=0,
        tiled=True,
    )
    new_latent = latent_sum.astype(jnp.bfloat16)
    attended = attend(queries, kv_cache, lengths, new_latent, KV)
    return (moe_out, new_latent, attended)


def solution(mesh):
    in_specs = (
        P(("sec", "dev"), None),
        P(("sec", "dev"), None),
        P(("sec", "dev"), None),
        P(None, ("sec", "dev")),
        P(None, ("sec", "dev")),
        P(("sec", "dev"), None),
        P(),
        P("dev", None),
        P(("sec", "dev"), None, None),
        P(("sec", "dev"), None, None),
        P(("sec", "dev")),
    )
    out_specs = (P(("sec", "dev"), None), P(("sec", "dev"), None), P(("sec", "dev"), None, None))
    pairwise = mesh.shape["sec"] == 2 and mesh.shape["dev"] == 2 << HIGH
    return jax.shard_map(
        per_device if pairwise else per_device_wide, mesh=mesh, in_specs=in_specs, out_specs=out_specs, check_vma=False
    )
```

```python
import jax
import jax.numpy as jnp
from jax import lax
from jax.experimental import pallas as pl
from jax.experimental.pallas import tpu as pltpu
from jax.sharding import PartitionSpec as P

FF = 2048
KV = 512
LANES = 128
CHUNK = 512
COLS = 896
CORE, LOW, MID, HIGH = 0, 1, 2, 3


score_scale = 192.0 ** (-0.5)
norm_eps = 1e-06


def swap(x, *bits):
    if bits == ("sec",):
        return lax.ppermute(x, "sec", [(i, i ^ 1) for i in range(lax.axis_size("sec"))])
    flips = sum(1 << bit for bit in bits)
    return lax.ppermute(x, "dev", [(i, i ^ flips) for i in range(lax.axis_size("dev"))])


def swap_both(x, bit):
    size = lax.axis_size("dev")
    pairs = [(i, i ^ (1 << bit) ^ size) for i in range(2 * size)]
    return lax.ppermute(x, ("sec", "dev"), pairs)


def wide_total(*parts):
    return sum(part.astype(jnp.float32) for part in parts)


def total(*parts):
    return wide_total(*parts).astype(jnp.bfloat16)


def cache_kernel(lengths_ref, q_ref, kv_ref, stats_ref, out_ref):
    heads, count = q_ref.shape[1], kv_ref.shape[2]
    lane = lax.broadcasted_iota(jnp.int32, (heads, LANES), 1)
    position = lax.broadcasted_iota(jnp.int32, (heads, count), 1)
    for row in range(q_ref.shape[0]):
        scores = jnp.dot(q_ref[row], kv_ref[row], preferred_element_type=jnp.float32) * score_scale
        scores = jnp.where(position < lengths_ref[row], scores, -1e30)
        peak = jnp.max(scores, axis=1, keepdims=True)
        spread = jnp.exp(scores - peak)
        denominator = jnp.sum(spread, axis=1, keepdims=True)
        out_ref[row] = lax.dot_general(
            spread.astype(jnp.bfloat16),
            kv_ref[row, :KV, :],
            (((1,), (1,)), ((), ())),
            preferred_element_type=jnp.float32,
        )
        stats_ref[row] = jnp.where(lane == 0, peak, denominator)


def cache_part(queries, kv_cache, lengths):
    rows, heads = queries.shape[:2]
    vmem = pl.BlockSpec(memory_space=pltpu.VMEM)
    return pl.pallas_call(
        cache_kernel,
        out_shape=(
            jax.ShapeDtypeStruct((rows, heads, LANES), jnp.float32),
            jax.ShapeDtypeStruct((rows, heads, KV), jnp.float32),
        ),
        in_specs=[pl.BlockSpec(memory_space=pltpu.SMEM), vmem, vmem],
        out_specs=[vmem] * 2,
        compiler_params=pltpu.CompilerParams(vmem_limit_bytes=8 << 20),
        cost_estimate=pl.CostEstimate(
            flops=4 * queries.size * kv_cache.shape[1],
            bytes_accessed=2 * kv_cache.size,
            transcendentals=0,
        ),
        name="cache_part",
    )(lengths, queries, jnp.swapaxes(kv_cache, 1, 2))


def kernel_call(body, out_shape, scalars, *arrays, name, mib, anywhere=0, scratch=()):
    vmem = pl.BlockSpec(memory_space=pltpu.VMEM)
    specs = [pl.BlockSpec(memory_space=pltpu.SMEM)] + [vmem] * (len(arrays) - anywhere)
    specs += [pl.BlockSpec(memory_space=pl.ANY)] * anywhere
    return pl.pallas_call(
        body,
        out_shape=out_shape,
        in_specs=specs,
        out_specs=jax.tree.map(lambda _: vmem, out_shape),
        scratch_shapes=scratch,
        compiler_params=pltpu.CompilerParams(vmem_limit_bytes=mib << 20),
        name=name,
    )(scalars, *arrays)


def with_info(hidden_in, expert_ids, gate_scores):
    picks = expert_ids.shape[1]
    values = (expert_ids.astype(jnp.bfloat16), gate_scores)
    info = sum(
        jnp.dot(v, jnp.eye(picks, LANES, i * picks, jnp.bfloat16), preferred_element_type=jnp.float32)
        for i, v in enumerate(values)
    )
    return jnp.concatenate([hidden_in, info.astype(hidden_in.dtype)], axis=1)


def pack_kernel(_, *refs):
    *blocks, out_ref = refs
    x = jnp.concatenate([block[...].astype(jnp.float32) for block in blocks], axis=0)
    out_ref[...] = x.astype(out_ref.dtype)


def pack_rows_of(*blocks):
    rows, width = blocks[0].shape
    out = jax.ShapeDtypeStruct((len(blocks) * rows, width), blocks[0].dtype)
    return kernel_call(
        pack_kernel, out, jnp.zeros((1,), jnp.int32), *blocks, name="pack_rows", mib=4
    )


def gather_rows(hidden_in, expert_ids, gate_scores, w_kv):
    x = with_info(hidden_in, expert_ids, gate_scores)
    high, mid, both = swap(x, HIGH), swap(x, MID), swap(x, MID, HIGH)
    mid, w_own = lax.optimization_barrier((mid, w_kv))
    x = pack_rows_of(x, high, mid, both)
    blocks = [x, swap(x, LOW), swap(x, "sec"), swap_both(x, LOW)]
    w_mid = swap(w_own, MID)
    return blocks + [swap(v, CORE) for v in blocks], w_mid


def experts_kernel(picks, place_ref, *refs):
    x_refs, w_refs, outs = refs[:8], refs[8:11], refs[11:15]
    gate_ref, up_ref, down_ref, sems = refs[15:]
    size, half = x_refs[0].shape
    half = (half - LANES) // 2
    moves = []
    for part in (pl.ds(0, half), pl.ds(half, half)):
        moves.append((w_refs[0].at[part], gate_ref.at[part]))
        moves.append((w_refs[1].at[part], up_ref.at[part]))
    for flip in range(2):
        part = pl.ds(pl.multiple_of((place_ref[2] ^ flip) * half, LANES), half)
        moves.append((w_refs[2].at[:, part], down_ref.at[:, part]))
    copies = [pltpu.make_async_copy(*move, sems.at[i]) for i, move in enumerate(moves)]
    for copy in copies:
        copy.start()

    def columns(cols):
        return jnp.concatenate([ref[:, cols] for ref in x_refs], axis=0)

    def ordered(x):
        n = size // 2
        parts = [x[i * n : (i + 1) * n] for i in range(x.shape[0] // n)]
        parts = [jnp.where(place_ref[2] == 1, pltpu.roll(v, n // 2, 0), v) for v in parts]
        done = []
        for i in range(0, len(parts), 4):
            for mid in range(2):
                pair = parts[i + mid], parts[i + 2 + mid]
                done.append(jnp.where(place_ref[1] == 1, pair[1], pair[0]))
                done.append(jnp.where(place_ref[1] == 1, pair[0], pair[1]))
        return jnp.concatenate(done, axis=0)

    info = columns(slice(2 * half, None)).astype(jnp.float32)
    rows, hid = info.shape[0], gate_ref.shape[1]
    lane = lax.broadcasted_iota(jnp.int32, info.shape, 1)
    scores = jnp.where(lane < picks, pltpu.roll(info, LANES - picks, 1), 0.0)
    named = jnp.where(info == place_ref[0].astype(jnp.float32), scores, 0.0)
    share = jnp.sum(named, axis=1, keepdims=True) / jnp.sum(scores, axis=1, keepdims=True)
    gate_act = jnp.zeros((rows, hid), jnp.float32)
    up_act = jnp.zeros((rows, hid), jnp.float32)
    for part in range(2):
        copies[2 * part].wait()
        copies[2 * part + 1].wait()
        for k in range(0, half, CHUNK):
            depth = slice(part * half + k, part * half + k + CHUNK)
            x = columns(depth)
            gate_act += jnp.dot(x, gate_ref[depth, :], preferred_element_type=jnp.float32)
            up_act += jnp.dot(x, up_ref[depth, :], preferred_element_type=jnp.float32)
    hidden = ordered(gate_act / (1.0 + jnp.exp(-gate_act)) * up_act).astype(jnp.bfloat16)
    share = ordered(jnp.broadcast_to(share, (rows, LANES)))[:, :1]
    block = half // 4
    for flip in range(2):
        copies[4 + flip].wait()
        for j in range(4):
            part, mid = j // 2, j % 2
            i = 2 * flip + mid
            kept, sent = outs[2 * part : 2 * part + 2]
            first = (place_ref[2] ^ flip) * half + mid * 2 * block + (place_ref[1] ^ part) * block
            for c in range(0, block, COLS):
                wide = min(COLS, block - c)
                cols = pl.ds(pl.multiple_of(first + c, LANES), wide)
                partial = jnp.dot(hidden, down_ref[:, cols], preferred_element_type=jnp.float32)
                partial = (partial * share).astype(jnp.bfloat16)
                to = slice(i * block + c, i * block + c + wide)
                kept[:, to] = partial[: rows // 2]
                sent[:, to] = partial[rows // 2 :]


def experts(place, blocks, picks, w_gate, w_up, w_down):
    out = jax.ShapeDtypeStruct((4 * blocks[0].shape[0], w_gate.shape[0] // 2), jnp.bfloat16)
    weights = (w_gate, w_up, w_down)
    return kernel_call(
        lambda *refs: experts_kernel(picks, *refs),
        (out,) * 4,
        place,
        *blocks,
        *weights,
        name="experts",
        mib=48,
        anywhere=3,
        scratch=[pltpu.VMEM(w.shape, w.dtype) for w in weights] + [pltpu.SemaphoreType.DMA((6,))],
    )


def scatter_rows(keep_a, send_a, keep_b, send_b, late):
    rows, cols = keep_a.shape[0] // 2, keep_a.shape[1] // 2
    here, there, left, right = slice(0, rows), slice(rows, None), slice(0, cols), slice(cols, None)
    b = [keep_b, swap(send_b, CORE)]
    a = [keep_a, swap(send_a, CORE)]
    ins = [
        swap(total(*(v[here] for v in b)), LOW),
        swap(total(*(v[there] for v in a)), "sec"),
        swap_both(total(*(v[there] for v in b)), LOW),
    ]
    a, ins, late = lax.optimization_barrier((a, ins, late))
    a += ins
    rows //= 2
    here, there = slice(0, rows), slice(rows, 2 * rows)
    ins = (
        swap(total(*(v[here, right] for v in a)), HIGH),
        swap(total(*(v[there, right] for v in a)), MID, HIGH),
        swap(total(*(v[there, left] for v in a)), MID),
    )
    return wide_total(*(v[here, left] for v in a)), ins, late


def residual_kernel(place_ref, own_ref, low_ref, out_ref):
    rows, cols = out_ref.shape
    n, block = rows // 2, cols // 2
    upper, odd = place_ref[2] == 1, place_ref[1] == 1
    pair = []
    for ref in (own_ref, low_ref):
        x = ref[:n].astype(jnp.float32)
        x = jnp.where(upper, x[:, 2 * cols : 4 * cols], x[:, : 2 * cols])
        pair.append(jnp.where(upper, pltpu.roll(x, n // 2, 0), x))
    pair = [jnp.where(odd, pair[1], pair[0]), jnp.where(odd, pair[0], pair[1])]
    x = jnp.concatenate(pair, axis=0)
    for mid in range(2):
        first = 2 * mid * block
        even = x[:, first : first + block]
        out_ref[:, mid * block : (mid + 1) * block] = jnp.where(
            odd, x[:, first + block : first + 2 * block], even
        )


def residual_rows(place, own, low):
    rows, width = own.shape
    out = jax.ShapeDtypeStruct((rows, (width - LANES) // 4), jnp.float32)
    return kernel_call(residual_kernel, out, place, own, low, name="residual_rows", mib=4)


OTHERS = ((1, 0), (0, 1), (1, 1))

def put_split(ref, first, apart, x):
    cols = x.shape[1]
    upper = x.astype(jnp.bfloat16)
    ref[:, first : first + cols] = upper
    rest = (x - upper.astype(jnp.float32)).astype(jnp.bfloat16)
    ref[:, first + apart : first + apart + cols] = rest


def get_split(ref, first, cols):
    upper = ref[:, first : first + cols].astype(jnp.float32)
    return upper + ref[:, first + cols : first + 2 * cols].astype(jnp.float32)


def latent_kernel(place_ref, sum_ref, residual_ref, gain_ref, *refs):
    in_refs, w_refs = refs[:3], refs[3:7]
    sums_ref, moe_ref, piece_ref = refs[7], refs[8], refs[12]
    rows, cols = sum_ref.shape
    block, n = cols // 2, rows // 4
    piece, lat = w_refs[0].shape


    def rows_for(x, low, high):
        x = jnp.where(place_ref[1] == 1 - low, x[2 * n :], x[: 2 * n])
        return jnp.where(place_ref[2] == 1 - high, x[n:], x[:n])

    mixture = sum_ref[...] + wide_total(*(ref[...] for ref in in_refs))
    moe = (residual_ref[...] + mixture).astype(jnp.bfloat16)
    widened = moe.astype(jnp.float32)
    for mid in range(2):
        first = (4 * place_ref[2] + 2 * mid + place_ref[1]) * block
        gain = gain_ref[:, pl.ds(pl.multiple_of(first, LANES), block)]
        scaled = widened[:, mid * block : (mid + 1) * block] * gain
        for core in range(2):
            piece_ref[2 * mid + core] = scaled[:, core * piece : (core + 1) * piece]
    sums = jnp.zeros((rows, lat), jnp.float32)
    for flips, w_ref in enumerate(w_refs):
        x = piece_ref[place_ref[3] ^ flips].astype(jnp.bfloat16)
        sums += jnp.dot(x, w_ref[...], preferred_element_type=jnp.float32)
    squares = jnp.sum(widened * widened, axis=1, keepdims=True)
    tail = jnp.broadcast_to(squares, (rows, LANES))
    wide = sums_ref.shape[1]
    tail = tail[:, : wide - lat]
    moe_ref[...] = rows_for(widened, 0, 0).astype(jnp.bfloat16)
    sums_ref[:, :lat] = rows_for(sums, 0, 0)
    sums_ref[:, lat:] = rows_for(tail, 0, 0)
    for (low, high), ref in zip(OTHERS, refs[9:12]):
        ref[:, :cols] = rows_for(widened, low, high).astype(jnp.bfloat16)
        put_split(ref, cols, wide, rows_for(sums, low, high))
        put_split(ref, cols + lat, wide, rows_for(tail, low, high))


def latent_parts(place, kept, received, residual, gain, slices):
    rows, cols = kept.shape
    piece, lat = slices[0].shape
    padded = -(-(lat + 1) // LANES) * LANES
    sums = jax.ShapeDtypeStruct((rows // 4, padded), jnp.float32)
    moe = jax.ShapeDtypeStruct((rows // 4, cols), jnp.bfloat16)
    sent = jax.ShapeDtypeStruct((rows // 4, cols + 2 * padded), jnp.bfloat16)
    return kernel_call(
        latent_kernel,
        (sums, moe, sent, sent, sent),
        place,
        kept,
        residual,
        gain,
        *received,
        *slices,
        name="latent_parts",
        mib=32,
        scratch=[pltpu.VMEM((4, rows, piece), jnp.float32)],
    )


def put_rows(place_ref, blocks, out_ref):
    cols = blocks[0][0].shape[1]
    block = cols // 2
    for high in range(2):
        parts = [jnp.where(place_ref[2] == high, x[0], x[1]) for x in blocks]
        for low in range(2):
            x = jnp.where(place_ref[1] == low, parts[0], parts[1])
            for mid in range(2):
                first = 2 * high * cols + mid * cols + low * block
                out_ref[:, first : first + block] = x[:, mid * block : (mid + 1) * block]


def finish_kernel(place_ref, sums_ref, moe_ref, q_ref, stats_ref, part_ref, *refs):
    in_refs, (moe_out, latent_ref, out_ref) = refs[:3], refs[3:]
    lat, cols = q_ref.shape[2], moe_ref.shape[1]
    sums = sums_ref[...]
    for ref in in_refs:
        sums += get_split(ref, cols, sums_ref.shape[1])
    inverse = lax.rsqrt(sums[:, lat : lat + 1] / (4 * cols) + norm_eps)
    rounded = (sums[:, :lat] * inverse).astype(jnp.bfloat16)
    latent_ref[...] = rounded
    latent = rounded.astype(jnp.float32)
    for row in range(q_ref.shape[0]):
        own = latent[row : row + 1]
        own_score = jnp.sum(q_ref[row].astype(jnp.float32) * own, axis=1, keepdims=True) * score_scale
        peak, denominator = stats_ref[row, :, 0:1], stats_ref[row, :, 1:2]
        top = jnp.maximum(peak, own_score)
        shrink = jnp.exp(peak - top)
        own_weight = jnp.exp(own_score - top)
        scale = 1.0 / (denominator * shrink + own_weight)
        own_prob = (own_weight * scale).astype(jnp.bfloat16).astype(jnp.float32)
        value = part_ref[row] * (shrink * scale) + own_prob * own[:, :KV]
        out_ref[row] = value.astype(jnp.bfloat16)
    other_low, other_high, other_both = (ref[:, :cols] for ref in in_refs)
    put_rows(place_ref, ((moe_ref[...], other_high), (other_low, other_both)), moe_out)


def finish(place, sums, moe, received, queries, stats, combined):
    rows, heads, lat = queries.shape
    outs = ((rows, 4 * moe.shape[1]), (rows, lat), (rows, heads, KV))
    return kernel_call(
        finish_kernel,
        tuple(jax.ShapeDtypeStruct(shape, jnp.bfloat16) for shape in outs),
        place,
        sums,
        moe,
        queries,
        stats,
        combined,
        *received,
        name="finish",
        mib=8,
    )


def per_device(
    hidden_in,
    expert_ids,
    gate_scores,
    w_gate,
    w_up,
    w_down,
    norm_gain,
    w_kv,
    queries,
    kv_cache,
    lengths,
):
    devices = lax.axis_size("dev")
    device = lax.axis_index("dev")
    shard_count = FF // w_gate.shape[1]
    expert = lax.axis_index("sec") * (devices // shard_count) + device // shard_count
    picks = expert_ids.shape[1]
    core_mid = (((device >> MID) & 1) << 1) | (device & 1)
    place = jnp.stack([expert, (device >> LOW) & 1, (device >> HIGH) & 1, core_mid])

    cache = cache_part(queries, kv_cache, lengths)
    blocks, w_mid = gather_rows(hidden_in, expert_ids, gate_scores, w_kv)
    partial = experts(place, blocks, picks, w_gate, w_up, w_down)
    partial, w_mid = lax.optimization_barrier((partial, w_mid))
    kept, received, late = scatter_rows(*partial, (cache,))
    (cache,) = late
    stats, combined = cache
    residual = residual_rows(place, blocks[0], blocks[1])
    gain = norm_gain.reshape(1, -1)
    slices = (w_kv, swap(w_kv, CORE), w_mid, swap(w_mid, CORE))
    sums, moe, *sent = latent_parts(place, kept, received, residual, gain, slices)
    bits = ((LOW,), (HIGH,), (LOW, HIGH))
    received = {i: swap(sent[i], *bits[i]) for i in (1, 2, 0)}
    received = [received[i] for i in range(3)]
    return finish(place, sums, moe, received, queries, stats, combined)


def shifted(x, axis, by):
    length = lax.axis_size(axis)
    return lax.ppermute(x, axis, [(i, (i + by) % length) for i in range(length)])


def attend(queries, kv_cache, lengths, latent_new, value_width):
    length_max = kv_cache.shape[1]
    scores = (
        jnp.einsum("bhl,bpl->bhp", queries, kv_cache, preferred_element_type=jnp.float32)
        * score_scale
    )
    visible = jnp.arange(length_max, dtype=jnp.int32)[None, None, :] < lengths[:, None, None]
    scores = jnp.where(visible, scores, -1e30)
    own_score = (
        jnp.einsum("bhl,bl->bh", queries, latent_new, preferred_element_type=jnp.float32)
        * score_scale
    )
    peak = jnp.maximum(jnp.max(scores, axis=2), own_score)
    spread = jnp.exp(scores - peak[:, :, None])
    own_weight = jnp.exp(own_score - peak)
    denominator = jnp.sum(spread, axis=2) + own_weight
    cache_weights = (spread / denominator[:, :, None]).astype(jnp.bfloat16)
    own_prob = (own_weight / denominator).astype(jnp.bfloat16)
    values = kv_cache[:, :, :value_width]
    combined = jnp.einsum("bhp,bpv->bhv", cache_weights, values, preferred_element_type=jnp.float32)
    combined = combined + own_prob.astype(jnp.float32)[:, :, None] * latent_new[
        :, None, :value_width
    ].astype(jnp.float32)
    return combined.astype(jnp.bfloat16)


def route_tables(expert_ids, gate_scores, section, per_section, total_experts, capacity):
    row_count, pick_count = expert_ids.shape
    weights = gate_scores.astype(jnp.float32)
    weights = weights / jnp.sum(weights, axis=1, keepdims=True)
    flat_ids = expert_ids.reshape(-1)
    onehot = (flat_ids[:, None] == jnp.arange(total_experts, dtype=jnp.int32)[None, :]).astype(
        jnp.int32
    )
    before = jnp.cumsum(onehot, axis=0) - onehot
    position = jnp.sum(before * onehot, axis=1)
    local_ids = flat_ids - section * per_section
    matches = (
        local_ids[None, None, :] == jnp.arange(per_section, dtype=jnp.int32)[:, None, None]
    ) & (position[None, None, :] == jnp.arange(capacity, dtype=jnp.int32)[None, :, None])
    matches = matches.reshape(per_section, capacity, row_count, pick_count)
    members = jnp.sum(matches.astype(jnp.float32), axis=3).astype(jnp.bfloat16)
    shares = jnp.sum(jnp.where(matches, weights[None, None], 0.0), axis=3)
    return (members, shares)


def pack_rows(members, rows_in, shard_count):
    per_section, capacity = (members.shape[0], members.shape[1])
    packed = jnp.einsum("ecb,bd->ecd", members, rows_in, preferred_element_type=jnp.float32).astype(
        jnp.bfloat16
    )
    widened = jnp.broadcast_to(
        packed[:, None], (per_section, shard_count, capacity, rows_in.shape[1])
    )
    return widened.reshape(per_section * shard_count, capacity, rows_in.shape[1])


def unpack(returned, shares, shard_count):
    per_section, capacity = (shares.shape[0], shares.shape[1])
    summed = jnp.sum(
        returned.astype(jnp.float32).reshape(per_section, shard_count, capacity, returned.shape[2]),
        axis=1,
    )
    return jnp.einsum("ecb,ecd->bd", shares, summed, precision=lax.Precision.HIGHEST)


def run_expert(slots, w_gate, w_up, w_down):
    flat_rows = slots.reshape(-1, slots.shape[-1])
    gate_act = jnp.dot(flat_rows, w_gate, preferred_element_type=jnp.float32)
    up_act = jnp.dot(flat_rows, w_up, preferred_element_type=jnp.float32)
    hidden = (jax.nn.silu(gate_act) * up_act).astype(jnp.bfloat16)
    partial_value = jnp.dot(hidden, w_down, preferred_element_type=jnp.float32).astype(jnp.bfloat16)
    return partial_value.reshape(slots.shape)


def per_device_wide(
    hidden_in,
    expert_ids,
    gate_scores,
    w_gate,
    w_up,
    w_down,
    norm_gain,
    w_kv,
    queries,
    kv_cache,
    lengths,
):
    sections = lax.axis_size("sec")
    devices = lax.axis_size("dev")
    section = lax.axis_index("sec")
    shard_count = FF // w_gate.shape[1]
    per_section = devices // shard_count
    total_experts = sections * per_section
    row_count, pick_count = expert_ids.shape
    capacity = max(2, (2 * row_count * pick_count + total_experts - 1) // total_experts)
    tables = [
        route_tables(
            expert_ids,
            gate_scores,
            (section + offset) % sections,
            per_section,
            total_experts,
            capacity,
        )
        for offset in range(2)
    ]
    outgoing = jnp.stack(
        [pack_rows(tables[offset][0], hidden_in, shard_count) for offset in range(2)]
    )
    incoming = lax.all_to_all(outgoing, "dev", split_axis=1, concat_axis=1, tiled=True)
    crossed = shifted(incoming[1], "sec", 1)
    local_slots = jnp.stack([incoming[0], crossed])
    results = run_expert(local_slots, w_gate, w_up, w_down)
    returned = shifted(results[1], "sec", 1)
    sending = jnp.stack([results[0], returned])
    back = lax.all_to_all(sending, "dev", split_axis=1, concat_axis=1, tiled=True)
    mixture = unpack(back[0], tables[0][1], shard_count) + unpack(
        back[1], tables[1][1], shard_count
    )
    moe_out = (hidden_in.astype(jnp.float32) + mixture).astype(jnp.bfloat16)
    widened = moe_out.astype(jnp.float32)
    normed = (
        widened
        * lax.rsqrt(jnp.mean(widened * widened, axis=1, keepdims=True) + norm_eps)
        * norm_gain
    ).astype(jnp.bfloat16)
    pieces = lax.all_to_all(normed, "dev", split_axis=1, concat_axis=0, tiled=True)
    latent_sum = lax.psum_scatter(
        jnp.dot(pieces, w_kv, preferred_element_type=jnp.float32),
        "dev",
        scatter_dimension=0,
        tiled=True,
    )
    new_latent = latent_sum.astype(jnp.bfloat16)
    attended = attend(queries, kv_cache, lengths, new_latent, KV)
    return (moe_out, new_latent, attended)


def solution(mesh):
    in_specs = (
        P(("sec", "dev"), None),
        P(("sec", "dev"), None),
        P(("sec", "dev"), None),
        P(None, ("sec", "dev")),
        P(None, ("sec", "dev")),
        P(("sec", "dev"), None),
        P(),
        P("dev", None),
        P(("sec", "dev"), None, None),
        P(("sec", "dev"), None, None),
        P(("sec", "dev")),
    )
    out_specs = (P(("sec", "dev"), None), P(("sec", "dev"), None), P(("sec", "dev"), None, None))
    pairwise = mesh.shape["sec"] == 2 and mesh.shape["dev"] == 2 << HIGH
    return jax.shard_map(
        per_device if pairwise else per_device_wide, mesh=mesh, in_specs=in_specs, out_specs=out_specs, check_vma=False
    )
```

```python
import jax
import jax.numpy as jnp
from jax import lax
from jax.experimental import pallas as pl
from jax.experimental.pallas import tpu as pltpu
from jax.sharding import PartitionSpec as P

FF = 2048
KV = 512
LANES = 128
CHUNK = 512
COLS = 896
CORE, LOW, MID, HIGH = 0, 1, 2, 3


score_scale = 192.0 ** (-0.5)
norm_eps = 1e-06


def swap(x, *bits):
    if bits == ("sec",):
        return lax.ppermute(x, "sec", [(i, i ^ 1) for i in range(lax.axis_size("sec"))])
    flips = sum(1 << bit for bit in bits)
    return lax.ppermute(x, "dev", [(i, i ^ flips) for i in range(lax.axis_size("dev"))])


def swap_both(x, bit):
    size = lax.axis_size("dev")
    pairs = [(i, i ^ (1 << bit) ^ size) for i in range(2 * size)]
    return lax.ppermute(x, ("sec", "dev"), pairs)


def wide_total(*parts):
    return sum(part.astype(jnp.float32) for part in parts)


def total(*parts):
    return wide_total(*parts).astype(jnp.bfloat16)


def cache_kernel(lengths_ref, q_ref, kv_ref, stats_ref, out_ref):
    heads, count = q_ref.shape[1], kv_ref.shape[2]
    lane = lax.broadcasted_iota(jnp.int32, (heads, LANES), 1)
    position = lax.broadcasted_iota(jnp.int32, (heads, count), 1)
    for row in range(q_ref.shape[0]):
        scores = jnp.dot(q_ref[row], kv_ref[row], preferred_element_type=jnp.float32) * score_scale
        scores = jnp.where(position < lengths_ref[row], scores, -1e30)
        peak = jnp.max(scores, axis=1, keepdims=True)
        spread = jnp.exp(scores - peak)
        denominator = jnp.sum(spread, axis=1, keepdims=True)
        out_ref[row] = lax.dot_general(
            spread.astype(jnp.bfloat16),
            kv_ref[row, :KV, :],
            (((1,), (1,)), ((), ())),
            preferred_element_type=jnp.float32,
        )
        stats_ref[row] = jnp.where(lane == 0, peak, denominator)


def cache_part(queries, kv_cache, lengths):
    rows, heads = queries.shape[:2]
    vmem = pl.BlockSpec(memory_space=pltpu.VMEM)
    return pl.pallas_call(
        cache_kernel,
        out_shape=(
            jax.ShapeDtypeStruct((rows, heads, LANES), jnp.float32),
            jax.ShapeDtypeStruct((rows, heads, KV), jnp.float32),
        ),
        in_specs=[pl.BlockSpec(memory_space=pltpu.SMEM), vmem, vmem],
        out_specs=[vmem] * 2,
        compiler_params=pltpu.CompilerParams(vmem_limit_bytes=8 << 20),
        cost_estimate=pl.CostEstimate(
            flops=4 * queries.size * kv_cache.shape[1],
            bytes_accessed=2 * kv_cache.size,
            transcendentals=0,
        ),
        name="cache_part",
    )(lengths, queries, jnp.swapaxes(kv_cache, 1, 2))


def kernel_call(body, out_shape, scalars, *arrays, name, mib, anywhere=0, scratch=()):
    vmem = pl.BlockSpec(memory_space=pltpu.VMEM)
    specs = [pl.BlockSpec(memory_space=pltpu.SMEM)] + [vmem] * (len(arrays) - anywhere)
    specs += [pl.BlockSpec(memory_space=pl.ANY)] * anywhere
    return pl.pallas_call(
        body,
        out_shape=out_shape,
        in_specs=specs,
        out_specs=jax.tree.map(lambda _: vmem, out_shape),
        scratch_shapes=scratch,
        compiler_params=pltpu.CompilerParams(vmem_limit_bytes=mib << 20),
        name=name,
    )(scalars, *arrays)


def with_info(hidden_in, expert_ids, gate_scores):
    picks = expert_ids.shape[1]
    values = (expert_ids.astype(jnp.bfloat16), gate_scores)
    info = sum(
        jnp.dot(v, jnp.eye(picks, LANES, i * picks, jnp.bfloat16), preferred_element_type=jnp.float32)
        for i, v in enumerate(values)
    )
    return jnp.concatenate([hidden_in, info.astype(hidden_in.dtype)], axis=1)


def pack_kernel(_, *refs):
    *blocks, out_ref = refs
    x = jnp.concatenate([block[...].astype(jnp.float32) for block in blocks], axis=0)
    out_ref[...] = x.astype(out_ref.dtype)


def pack_rows_of(*blocks):
    rows, width = blocks[0].shape
    out = jax.ShapeDtypeStruct((len(blocks) * rows, width), blocks[0].dtype)
    return kernel_call(
        pack_kernel, out, jnp.zeros((1,), jnp.int32), *blocks, name="pack_rows", mib=4
    )


def gather_rows(hidden_in, expert_ids, gate_scores, w_kv):
    x = with_info(hidden_in, expert_ids, gate_scores)
    high, mid, both = swap(x, HIGH), swap(x, MID), swap(x, MID, HIGH)
    mid, w_own = lax.optimization_barrier((mid, w_kv))
    x = pack_rows_of(x, high, mid, both)
    blocks = [x, swap(x, LOW), swap(x, "sec"), swap_both(x, LOW)]
    w_mid = swap(w_own, MID)
    return blocks + [swap(v, CORE) for v in blocks], w_mid


def experts_kernel(picks, place_ref, *refs):
    x_refs, w_refs, outs = refs[:8], refs[8:11], refs[11:15]
    gate_ref, up_ref, down_ref, sems = refs[15:]
    size, half = x_refs[0].shape
    half = (half - LANES) // 2
    moves = []
    for part in (pl.ds(0, half), pl.ds(half, half)):
        moves.append((w_refs[0].at[part], gate_ref.at[part]))
        moves.append((w_refs[1].at[part], up_ref.at[part]))
    for flip in range(2):
        part = pl.ds(pl.multiple_of((place_ref[2] ^ flip) * half, LANES), half)
        moves.append((w_refs[2].at[:, part], down_ref.at[:, part]))
    copies = [pltpu.make_async_copy(*move, sems.at[i]) for i, move in enumerate(moves)]
    for copy in copies:
        copy.start()

    def columns(cols):
        return jnp.concatenate([ref[:, cols] for ref in x_refs], axis=0)

    def ordered(x):
        n = size // 2
        parts = [x[i * n : (i + 1) * n] for i in range(x.shape[0] // n)]
        parts = [jnp.where(place_ref[2] == 1, pltpu.roll(v, n // 2, 0), v) for v in parts]
        done = []
        for i in range(0, len(parts), 4):
            for mid in range(2):
                pair = parts[i + mid], parts[i + 2 + mid]
                done.append(jnp.where(place_ref[1] == 1, pair[1], pair[0]))
                done.append(jnp.where(place_ref[1] == 1, pair[0], pair[1]))
        return jnp.concatenate(done, axis=0)

    info = columns(slice(2 * half, None)).astype(jnp.float32)
    rows, hid = info.shape[0], gate_ref.shape[1]
    lane = lax.broadcasted_iota(jnp.int32, info.shape, 1)
    scores = jnp.where(lane < picks, pltpu.roll(info, LANES - picks, 1), 0.0)
    named = jnp.where(info == place_ref[0].astype(jnp.float32), scores, 0.0)
    share = jnp.sum(named, axis=1, keepdims=True) / jnp.sum(scores, axis=1, keepdims=True)
    gate_act = jnp.zeros((rows, hid), jnp.float32)
    up_act = jnp.zeros((rows, hid), jnp.float32)
    for part in range(2):
        copies[2 * part].wait()
        copies[2 * part + 1].wait()
        for k in range(0, half, CHUNK):
            depth = slice(part * half + k, part * half + k + CHUNK)
            x = columns(depth)
            gate_act += jnp.dot(x, gate_ref[depth, :], preferred_element_type=jnp.float32)
            up_act += jnp.dot(x, up_ref[depth, :], preferred_element_type=jnp.float32)
    hidden = ordered(gate_act / (1.0 + jnp.exp(-gate_act)) * up_act).astype(jnp.bfloat16)
    share = ordered(jnp.broadcast_to(share, (rows, LANES)))[:, :1]
    block = half // 4
    for flip in range(2):
        copies[4 + flip].wait()
        for j in range(4):
            part, mid = j // 2, j % 2
            i = 2 * flip + mid
            kept, sent = outs[2 * part : 2 * part + 2]
            first = (place_ref[2] ^ flip) * half + mid * 2 * block + (place_ref[1] ^ part) * block
            for c in range(0, block, COLS):
                wide = min(COLS, block - c)
                cols = pl.ds(pl.multiple_of(first + c, LANES), wide)
                partial = jnp.dot(hidden, down_ref[:, cols], preferred_element_type=jnp.float32)
                partial = (partial * share).astype(jnp.bfloat16)
                to = slice(i * block + c, i * block + c + wide)
                kept[:, to] = partial[: rows // 2]
                sent[:, to] = partial[rows // 2 :]


def experts(place, blocks, picks, w_gate, w_up, w_down):
    out = jax.ShapeDtypeStruct((4 * blocks[0].shape[0], w_gate.shape[0] // 2), jnp.bfloat16)
    weights = (w_gate, w_up, w_down)
    return kernel_call(
        lambda *refs: experts_kernel(picks, *refs),
        (out,) * 4,
        place,
        *blocks,
        *weights,
        name="experts",
        mib=48,
        anywhere=3,
        scratch=[pltpu.VMEM(w.shape, w.dtype) for w in weights] + [pltpu.SemaphoreType.DMA((6,))],
    )


def scatter_rows(keep_a, send_a, keep_b, send_b, late):
    rows, cols = keep_a.shape[0] // 2, keep_a.shape[1] // 2
    here, there, left, right = slice(0, rows), slice(rows, None), slice(0, cols), slice(cols, None)
    b = [keep_b, swap(send_b, CORE)]
    a = [keep_a, swap(send_a, CORE)]
    ins = [
        swap(total(*(v[here] for v in b)), LOW),
        swap(total(*(v[there] for v in a)), "sec"),
        swap_both(total(*(v[there] for v in b)), LOW),
    ]
    a, ins, late = lax.optimization_barrier((a, ins, late))
    a += ins
    rows //= 2
    here, there = slice(0, rows), slice(rows, 2 * rows)
    ins = (
        swap(total(*(v[here, right] for v in a)), HIGH),
        swap(total(*(v[there, right] for v in a)), MID, HIGH),
        swap(total(*(v[there, left] for v in a)), MID),
    )
    return wide_total(*(v[here, left] for v in a)), ins, late


def residual_kernel(place_ref, own_ref, low_ref, out_ref):
    rows, cols = out_ref.shape
    n, block = rows // 2, cols // 2
    upper, odd = place_ref[2] == 1, place_ref[1] == 1
    pair = []
    for ref in (own_ref, low_ref):
        x = ref[:n].astype(jnp.float32)
        x = jnp.where(upper, x[:, 2 * cols : 4 * cols], x[:, : 2 * cols])
        pair.append(jnp.where(upper, pltpu.roll(x, n // 2, 0), x))
    pair = [jnp.where(odd, pair[1], pair[0]), jnp.where(odd, pair[0], pair[1])]
    x = jnp.concatenate(pair, axis=0)
    for mid in range(2):
        first = 2 * mid * block
        even = x[:, first : first + block]
        out_ref[:, mid * block : (mid + 1) * block] = jnp.where(
            odd, x[:, first + block : first + 2 * block], even
        )


def residual_rows(place, own, low):
    rows, width = own.shape
    out = jax.ShapeDtypeStruct((rows, (width - LANES) // 4), jnp.float32)
    return kernel_call(residual_kernel, out, place, own, low, name="residual_rows", mib=4)


OTHERS = ((1, 0), (0, 1), (1, 1))

def put_split(ref, first, apart, x):
    cols = x.shape[1]
    upper = x.astype(jnp.bfloat16)
    ref[:, first : first + cols] = upper
    rest = (x - upper.astype(jnp.float32)).astype(jnp.bfloat16)
    ref[:, first + apart : first + apart + cols] = rest


def get_split(ref, first, cols):
    upper = ref[:, first : first + cols].astype(jnp.float32)
    return upper + ref[:, first + cols : first + 2 * cols].astype(jnp.float32)


def latent_kernel(place_ref, sum_ref, residual_ref, gain_ref, *refs):
    in_refs, w_refs = refs[:3], refs[3:7]
    sums_ref, moe_ref, piece_ref = refs[7], refs[8], refs[12]
    rows, cols = sum_ref.shape
    block, n = cols // 2, rows // 4
    piece, lat = w_refs[0].shape


    def rows_for(x, low, high):
        x = jnp.where(place_ref[1] == 1 - low, x[2 * n :], x[: 2 * n])
        return jnp.where(place_ref[2] == 1 - high, x[n:], x[:n])

    mixture = sum_ref[...] + wide_total(*(ref[...] for ref in in_refs))
    moe = (residual_ref[...] + mixture).astype(jnp.bfloat16)
    widened = moe.astype(jnp.float32)
    for mid in range(2):
        first = (4 * place_ref[2] + 2 * mid + place_ref[1]) * block
        gain = gain_ref[:, pl.ds(pl.multiple_of(first, LANES), block)]
        scaled = widened[:, mid * block : (mid + 1) * block] * gain
        for core in range(2):
            piece_ref[2 * mid + core] = scaled[:, core * piece : (core + 1) * piece]
    sums = jnp.zeros((rows, lat), jnp.float32)
    for flips, w_ref in enumerate(w_refs):
        x = piece_ref[place_ref[3] ^ flips].astype(jnp.bfloat16)
        sums += jnp.dot(x, w_ref[...], preferred_element_type=jnp.float32)
    squares = jnp.sum(widened * widened, axis=1, keepdims=True)
    tail = jnp.broadcast_to(squares, (rows, LANES))
    wide = sums_ref.shape[1]
    tail = tail[:, : wide - lat]
    moe_ref[...] = rows_for(widened, 0, 0).astype(jnp.bfloat16)
    sums_ref[:, :lat] = rows_for(sums, 0, 0)
    sums_ref[:, lat:] = rows_for(tail, 0, 0)
    for (low, high), ref in zip(OTHERS, refs[9:12]):
        ref[:, :cols] = rows_for(widened, low, high).astype(jnp.bfloat16)
        put_split(ref, cols, wide, rows_for(sums, low, high))
        put_split(ref, cols + lat, wide, rows_for(tail, low, high))


def latent_parts(place, kept, received, residual, gain, slices):
    rows, cols = kept.shape
    piece, lat = slices[0].shape
    padded = -(-(lat + 1) // LANES) * LANES
    sums = jax.ShapeDtypeStruct((rows // 4, padded), jnp.float32)
    moe = jax.ShapeDtypeStruct((rows // 4, cols), jnp.bfloat16)
    sent = jax.ShapeDtypeStruct((rows // 4, cols + 2 * padded), jnp.bfloat16)
    return kernel_call(
        latent_kernel,
        (sums, moe, sent, sent, sent),
        place,
        kept,
        residual,
        gain,
        *received,
        *slices,
        name="latent_parts",
        mib=32,
        scratch=[pltpu.VMEM((4, rows, piece), jnp.float32)],
    )


def put_rows(place_ref, blocks, out_ref):
    cols = blocks[0][0].shape[1]
    block = cols // 2
    for high in range(2):
        parts = [jnp.where(place_ref[2] == high, x[0], x[1]) for x in blocks]
        for low in range(2):
            x = jnp.where(place_ref[1] == low, parts[0], parts[1])
            for mid in range(2):
                first = 2 * high * cols + mid * cols + low * block
                out_ref[:, first : first + block] = x[:, mid * block : (mid + 1) * block]


def finish_kernel(place_ref, sums_ref, moe_ref, q_ref, stats_ref, part_ref, *refs):
    in_refs, (moe_out, latent_ref, out_ref) = refs[:3], refs[3:]
    lat, cols = q_ref.shape[2], moe_ref.shape[1]
    sums = sums_ref[...]
    for ref in in_refs:
        sums += get_split(ref, cols, sums_ref.shape[1])
    inverse = lax.rsqrt(sums[:, lat : lat + 1] / (4 * cols) + norm_eps)
    rounded = (sums[:, :lat] * inverse).astype(jnp.bfloat16)
    latent_ref[...] = rounded
    latent = rounded.astype(jnp.float32)
    for row in range(q_ref.shape[0]):
        own = latent[row : row + 1]
        own_score = jnp.sum(q_ref[row].astype(jnp.float32) * own, axis=1, keepdims=True) * score_scale
        peak, denominator = stats_ref[row, :, 0:1], stats_ref[row, :, 1:2]
        top = jnp.maximum(peak, own_score)
        shrink = jnp.exp(peak - top)
        own_weight = jnp.exp(own_score - top)
        scale = 1.0 / (denominator * shrink + own_weight)
        own_prob = (own_weight * scale).astype(jnp.bfloat16).astype(jnp.float32)
        value = part_ref[row] * (shrink * scale) + own_prob * own[:, :KV]
        out_ref[row] = value.astype(jnp.bfloat16)
    other_low, other_high, other_both = (ref[:, :cols] for ref in in_refs)
    put_rows(place_ref, ((moe_ref[...], other_high), (other_low, other_both)), moe_out)


def finish(place, sums, moe, received, queries, stats, combined):
    rows, heads, lat = queries.shape
    outs = ((rows, 4 * moe.shape[1]), (rows, lat), (rows, heads, KV))
    return kernel_call(
        finish_kernel,
        tuple(jax.ShapeDtypeStruct(shape, jnp.bfloat16) for shape in outs),
        place,
        sums,
        moe,
        queries,
        stats,
        combined,
        *received,
        name="finish",
        mib=8,
    )


def per_device(
    hidden_in,
    expert_ids,
    gate_scores,
    w_gate,
    w_up,
    w_down,
    norm_gain,
    w_kv,
    queries,
    kv_cache,
    lengths,
):
    devices = lax.axis_size("dev")
    device = lax.axis_index("dev")
    shard_count = FF // w_gate.shape[1]
    expert = lax.axis_index("sec") * (devices // shard_count) + device // shard_count
    picks = expert_ids.shape[1]
    core_mid = (((device >> MID) & 1) << 1) | (device & 1)
    place = jnp.stack([expert, (device >> LOW) & 1, (device >> HIGH) & 1, core_mid])

    cache = cache_part(queries, kv_cache, lengths)
    blocks, w_mid = gather_rows(hidden_in, expert_ids, gate_scores, w_kv)
    partial = experts(place, blocks, picks, w_gate, w_up, w_down)
    partial, w_mid = lax.optimization_barrier((partial, w_mid))
    kept, received, late = scatter_rows(*partial, ())
    del late
    stats, combined = cache
    residual = residual_rows(place, blocks[0], blocks[1])
    gain = norm_gain.reshape(1, -1)
    slices = (w_kv, swap(w_kv, CORE), w_mid, swap(w_mid, CORE))
    sums, moe, *sent = latent_parts(place, kept, received, residual, gain, slices)
    bits = ((LOW,), (HIGH,), (LOW, HIGH))
    received = {i: swap(sent[i], *bits[i]) for i in (1, 2, 0)}
    received = [received[i] for i in range(3)]
    return finish(place, sums, moe, received, queries, stats, combined)


def shifted(x, axis, by):
    length = lax.axis_size(axis)
    return lax.ppermute(x, axis, [(i, (i + by) % length) for i in range(length)])


def attend(queries, kv_cache, lengths, latent_new, value_width):
    length_max = kv_cache.shape[1]
    scores = (
        jnp.einsum("bhl,bpl->bhp", queries, kv_cache, preferred_element_type=jnp.float32)
        * score_scale
    )
    visible = jnp.arange(length_max, dtype=jnp.int32)[None, None, :] < lengths[:, None, None]
    scores = jnp.where(visible, scores, -1e30)
    own_score = (
        jnp.einsum("bhl,bl->bh", queries, latent_new, preferred_element_type=jnp.float32)
        * score_scale
    )
    peak = jnp.maximum(jnp.max(scores, axis=2), own_score)
    spread = jnp.exp(scores - peak[:, :, None])
    own_weight = jnp.exp(own_score - peak)
    denominator = jnp.sum(spread, axis=2) + own_weight
    cache_weights = (spread / denominator[:, :, None]).astype(jnp.bfloat16)
    own_prob = (own_weight / denominator).astype(jnp.bfloat16)
    values = kv_cache[:, :, :value_width]
    combined = jnp.einsum("bhp,bpv->bhv", cache_weights, values, preferred_element_type=jnp.float32)
    combined = combined + own_prob.astype(jnp.float32)[:, :, None] * latent_new[
        :, None, :value_width
    ].astype(jnp.float32)
    return combined.astype(jnp.bfloat16)


def route_tables(expert_ids, gate_scores, section, per_section, total_experts, capacity):
    row_count, pick_count = expert_ids.shape
    weights = gate_scores.astype(jnp.float32)
    weights = weights / jnp.sum(weights, axis=1, keepdims=True)
    flat_ids = expert_ids.reshape(-1)
    onehot = (flat_ids[:, None] == jnp.arange(total_experts, dtype=jnp.int32)[None, :]).astype(
        jnp.int32
    )
    before = jnp.cumsum(onehot, axis=0) - onehot
    position = jnp.sum(before * onehot, axis=1)
    local_ids = flat_ids - section * per_section
    matches = (
        local_ids[None, None, :] == jnp.arange(per_section, dtype=jnp.int32)[:, None, None]
    ) & (position[None, None, :] == jnp.arange(capacity, dtype=jnp.int32)[None, :, None])
    matches = matches.reshape(per_section, capacity, row_count, pick_count)
    members = jnp.sum(matches.astype(jnp.float32), axis=3).astype(jnp.bfloat16)
    shares = jnp.sum(jnp.where(matches, weights[None, None], 0.0), axis=3)
    return (members, shares)


def pack_rows(members, rows_in, shard_count):
    per_section, capacity = (members.shape[0], members.shape[1])
    packed = jnp.einsum("ecb,bd->ecd", members, rows_in, preferred_element_type=jnp.float32).astype(
        jnp.bfloat16
    )
    widened = jnp.broadcast_to(
        packed[:, None], (per_section, shard_count, capacity, rows_in.shape[1])
    )
    return widened.reshape(per_section * shard_count, capacity, rows_in.shape[1])


def unpack(returned, shares, shard_count):
    per_section, capacity = (shares.shape[0], shares.shape[1])
    summed = jnp.sum(
        returned.astype(jnp.float32).reshape(per_section, shard_count, capacity, returned.shape[2]),
        axis=1,
    )
    return jnp.einsum("ecb,ecd->bd", shares, summed, precision=lax.Precision.HIGHEST)


def run_expert(slots, w_gate, w_up, w_down):
    flat_rows = slots.reshape(-1, slots.shape[-1])
    gate_act = jnp.dot(flat_rows, w_gate, preferred_element_type=jnp.float32)
    up_act = jnp.dot(flat_rows, w_up, preferred_element_type=jnp.float32)
    hidden = (jax.nn.silu(gate_act) * up_act).astype(jnp.bfloat16)
    partial_value = jnp.dot(hidden, w_down, preferred_element_type=jnp.float32).astype(jnp.bfloat16)
    return partial_value.reshape(slots.shape)


def per_device_wide(
    hidden_in,
    expert_ids,
    gate_scores,
    w_gate,
    w_up,
    w_down,
    norm_gain,
    w_kv,
    queries,
    kv_cache,
    lengths,
):
    sections = lax.axis_size("sec")
    devices = lax.axis_size("dev")
    section = lax.axis_index("sec")
    shard_count = FF // w_gate.shape[1]
    per_section = devices // shard_count
    total_experts = sections * per_section
    row_count, pick_count = expert_ids.shape
    capacity = max(2, (2 * row_count * pick_count + total_experts - 1) // total_experts)
    tables = [
        route_tables(
            expert_ids,
            gate_scores,
            (section + offset) % sections,
            per_section,
            total_experts,
            capacity,
        )
        for offset in range(2)
    ]
    outgoing = jnp.stack(
        [pack_rows(tables[offset][0], hidden_in, shard_count) for offset in range(2)]
    )
    incoming = lax.all_to_all(outgoing, "dev", split_axis=1, concat_axis=1, tiled=True)
    crossed = shifted(incoming[1], "sec", 1)
    local_slots = jnp.stack([incoming[0], crossed])
    results = run_expert(local_slots, w_gate, w_up, w_down)
    returned = shifted(results[1], "sec", 1)
    sending = jnp.stack([results[0], returned])
    back = lax.all_to_all(sending, "dev", split_axis=1, concat_axis=1, tiled=True)
    mixture = unpack(back[0], tables[0][1], shard_count) + unpack(
        back[1], tables[1][1], shard_count
    )
    moe_out = (hidden_in.astype(jnp.float32) + mixture).astype(jnp.bfloat16)
    widened = moe_out.astype(jnp.float32)
    normed = (
        widened
        * lax.rsqrt(jnp.mean(widened * widened, axis=1, keepdims=True) + norm_eps)
        * norm_gain
    ).astype(jnp.bfloat16)
    pieces = lax.all_to_all(normed, "dev", split_axis=1, concat_axis=0, tiled=True)
    latent_sum = lax.psum_scatter(
        jnp.dot(pieces, w_kv, preferred_element_type=jnp.float32),
        "dev",
        scatter_dimension=0,
        tiled=True,
    )
    new_latent = latent_sum.astype(jnp.bfloat16)
    attended = attend(queries, kv_cache, lengths, new_latent, KV)
    return (moe_out, new_latent, attended)


def solution(mesh):
    in_specs = (
        P(("sec", "dev"), None),
        P(("sec", "dev"), None),
        P(("sec", "dev"), None),
        P(None, ("sec", "dev")),
        P(None, ("sec", "dev")),
        P(("sec", "dev"), None),
        P(),
        P("dev", None),
        P(("sec", "dev"), None, None),
        P(("sec", "dev"), None, None),
        P(("sec", "dev")),
    )
    out_specs = (P(("sec", "dev"), None), P(("sec", "dev"), None), P(("sec", "dev"), None, None))
    pairwise = mesh.shape["sec"] == 2 and mesh.shape["dev"] == 2 << HIGH
    return jax.shard_map(
        per_device if pairwise else per_device_wide, mesh=mesh, in_specs=in_specs, out_specs=out_specs, check_vma=False
    )
```
